128 devices in a mesh: level: 4 (over x), grp: 32 (over z, y, core).
Axes of the slice: x: 4, y: 4, z: 4, core: 2. Of those that a mesh axis runs over, the one named last changes fastest.
Arguments:
- x_old: bfloat16 [4, 512, 16, 128], P('level', 'grp'), may hold values from -6 to 6
- rhs: float32 [4, 512, 16, 128], P('level', 'grp'), may hold values from -6 to 6
- down_tiles: bfloat16 [4, 512, 6, 128, 128], P('level', 'grp'), may hold values from -0.4375 to 0.4375
- level_tiles: bfloat16 [4, 512, 6, 128, 128], P('level', 'grp'), may hold values from -0.1875 to 0.1875
- up_tiles: bfloat16 [4, 512, 6, 128, 128], P('level', 'grp'), may hold values from -0.1875 to 0.1875
- inverses: float32 [4, 512, 128, 128], P('level', 'grp'), as said below
- tile_cols: int32 [4, 512, 3, 6], P('level', 'grp'), may hold values from 0 to 511
- tile_counts: int32 [4, 512, 3], P('level', 'grp'), may hold values from 1 to 6, as said below
Outputs:
- solution: float32 [4, 512, 16, 128], P('level', 'grp')
The draws below stay inside these ranges and needn't reach their ends.
Inputs may be any that keep to these rules, and one draw needn't show every extreme that they name: `tile_counts`: slots at or beyond a block row's count are to be ignored; every level has a block row with 6 live slots in every band. `inverses`: each inverse is an arbitrary dense matrix given in full.
All inputs are finite; a program needn't handle non-finite values.
Results may differ from the reference program's by a relative error of at most 0.0015.
Values may be sent and summed in bfloat16 or wider, within the bound.
A program may use at most 64 MiB of HBM per device.

```python
import jax
import jax.numpy as jnp
from jax import lax

TILE = 128
R = 16
K = 6
NBL = 512
LEVELS = 4


def draw_inverses(key, part):
    first, second = jax.random.split(key)
    diag_part = jax.random.uniform(first, (LEVELS, NBL, TILE), jnp.float32, 0.6, 1.0)
    rest = jax.random.normal(second, (LEVELS, NBL, TILE, TILE), jnp.float32) * (0.3 / TILE ** 0.5)
    eye = jnp.eye(TILE, dtype=jnp.float32)
    return rest * (1.0 - eye) + diag_part[:, :, :, None] * eye


def draw_tile_counts(key, part):
    counts = jax.random.randint(key, (LEVELS, NBL, 3), 1, K + 1).astype(jnp.int32)
    rows = jnp.arange(NBL, dtype=jnp.int32)
    chosen = jnp.arange(LEVELS, dtype=jnp.int32) * 7 % NBL
    full = rows[None, :, None] == chosen[:, None, None]
    return jnp.where(full, jnp.int32(K), counts)


def plant(drawn, stream_key, least, high):
    extent = drawn.shape
    place = [jax.random.randint(jax.random.fold_in(stream_key, axis), (), 0, extent[axis]) for axis in range(len(extent))]
    drawn = drawn.at[tuple(place)].set(least)
    longest = extent.index(max(extent))
    place[longest] = (place[longest] + 1) % extent[longest]
    return drawn.at[tuple(place)].set(high)


def level_of(key, shape, cuts, low, high):
    loudness, own = 1.0, jax.random.fold_in(key, 6)
    for dim, blocks in cuts:
        draws = jnp.exp(jax.random.uniform(jax.random.fold_in(own, dim), (blocks,), jnp.float32, low / len(cuts), high / len(cuts)))
        loudness = loudness * jnp.repeat(draws, shape[dim] // blocks).reshape([-1 if axis == dim else 1 for axis in range(len(shape))])
    return loudness


def noise(own_key, shape, width, limit, cuts=(), held_as=jnp.bfloat16):
    values = jax.random.normal(own_key, shape, jnp.float32) * width
    if len(cuts) > 0:
        values = level_of(own_key, shape, cuts, -0.22, 0.18) * values
    return jnp.clip(values, min=-limit, max=limit).astype(held_as)


def setup_inputs(seed: int = 0) -> dict:
    keys = jax.random.split(jax.random.key(seed), 9)
    x_old = noise(keys[0], (LEVELS, NBL, R, TILE), 1.0, 6.0, ((0, 4), (1, 32)))
    rhs = noise(keys[1], (LEVELS, NBL, R, TILE), 1.0, 6.0, ((0, 4), (1, 32)), jnp.float32)
    down_tiles = noise(keys[2], (LEVELS, NBL, K, TILE, TILE), (0.8 / (TILE * K) ** 0.5), 0.4375, ((0, 4), (1, 32)))
    level_tiles = noise(keys[3], (LEVELS, NBL, K, TILE, TILE), (0.35 / (TILE * K) ** 0.5), 0.1875, ((0, 4), (1, 32)))
    up_tiles = noise(keys[4], (LEVELS, NBL, K, TILE, TILE), (0.35 / (TILE * K) ** 0.5), 0.1875, ((0, 4), (1, 32)))
    inverses = draw_inverses(jax.random.fold_in(keys[8], 71), 0)
    tile_cols = plant(jax.random.randint(keys[6], (LEVELS, NBL, 3, K), 0, NBL), jax.random.fold_in(keys[6], 1), 0, NBL - 1).astype(jnp.int32)
    tile_counts = draw_tile_counts(jax.random.fold_in(keys[8], 71), 0)
    return dict(x_old=x_old, rhs=rhs, down_tiles=down_tiles, level_tiles=level_tiles, up_tiles=up_tiles, inverses=inverses, tile_cols=tile_cols, tile_counts=tile_counts)


def band_term(tiles, cols, counts, source):
    pieces = source[cols].astype(jnp.float32)
    slots = jnp.arange(cols.shape[1], dtype=jnp.int32)
    live = slots[None, :] < counts[:, None]
    pieces = jnp.where(live[:, :, None, None], pieces, 0.0)
    return jnp.einsum("bkrc,bkcq->brq", pieces, tiles.astype(jnp.float32))


def reference(x_old, rhs, down_tiles, level_tiles, up_tiles, inverses, tile_cols, tile_counts):
    above_old = jnp.concatenate([x_old[1:], jnp.zeros_like(x_old[:1])], axis=0)

    def level_step(carry, items):
        rhs_l, down_l, same_l, up_l, inv_l, cols_l, counts_l, own_l, above_l = items
        base = rhs_l - band_term(same_l, cols_l[:, 1], counts_l[:, 1], own_l)
        base = base - band_term(up_l, cols_l[:, 2], counts_l[:, 2], above_l)
        resid = base - band_term(down_l, cols_l[:, 0], counts_l[:, 0], carry)
        result = jnp.einsum("brc,bcq->brq", resid, inv_l.astype(jnp.float32), precision=lax.Precision.HIGHEST)
        return result.astype(jnp.bfloat16), result

    start = jnp.zeros(x_old.shape[1:], jnp.bfloat16)
    _, solution = lax.scan(level_step, start, (rhs, down_tiles, level_tiles, up_tiles, inverses, tile_cols, tile_counts, x_old, above_old))
    return solution
```

```python
import functools

import jax
import jax.numpy as jnp
from jax import lax
from jax.experimental import pallas as pl
from jax.experimental.pallas import tpu as pltpu
from jax.sharding import PartitionSpec as P

MESH = pl.DeviceIdType.MESH
ROWS = 16
SLOTS = 6
TILE = 128
LEVELS = 4
PARTS = 2
WIDTH = ROWS // PARTS
SHARD = ROWS // PARTS
GROUP = 4 * SHARD
HALF = 16 * SHARD
OWN, ABOVE, DOWN = 1, 2, 0
F32, BF16 = jnp.float32, jnp.bfloat16


def fold(total):
    while total.shape[0] > WIDTH:
        half = total.shape[0] // 2
        total = total[:half] + total[half:]
    return total


def sweep(x_hbm, rhs_hbm, down_hbm, level_hbm, up_hbm, inv_hbm, cols, counts, out_hbm, *scratch):
    panels = {
        OWN: scratch[:PARTS],
        ABOVE: scratch[PARTS : 2 * PARTS],
        DOWN: scratch[2 * PARTS : 3 * PARTS],
    }
    outgoing = scratch[3 * PARTS : 4 * PARTS]
    results = scratch[4 * PARTS : 5 * PARTS]
    bases = scratch[5 * PARTS : 6 * PARTS]
    (x_vmem, rhs_vmem, down, level_t, up, inv, inv_split, masks, place, pick, load_sem, out_sem, send_sem, recv_sem) = scratch[6 * PARTS :]

    level = lax.axis_index("level")
    grp = lax.axis_index("grp")
    core = lax.rem(grp, 2)
    y = lax.rem(lax.div(grp, 2), 4)
    z = lax.div(grp, 8)
    first = core == 0
    a = jnp.where(first, y, z)
    b = jnp.where(first, z, y)
    lower = lax.rem(level + LEVELS - 1, LEVELS)
    upper = lax.rem(level + 1, LEVELS)

    def device(at_level, at_a, at_b):
        at_y = jnp.where(first, at_a, at_b)
        at_z = jnp.where(first, at_b, at_a)
        return (at_level, at_z * 8 + at_y * 2 + core)

    sibling = (level, z * 8 + y * 2 + 1 - core)

    def turn(value, by):
        return lax.rem(value + by, 4)

    loads = [
        (x_hbm.at[0], x_vmem),
        (level_hbm.at[0], level_t),
        (up_hbm.at[0], up),
        (rhs_hbm.at[0], rhs_vmem),
        (inv_hbm.at[0], inv),
        (down_hbm.at[0], down),
    ]
    loads = [pltpu.make_async_copy(src, dst, load_sem.at[n]) for n, (src, dst) in enumerate(loads)]
    for load in loads:
        load.start()

    barrier = pltpu.get_barrier_semaphore()
    partners = [sibling]
    partners += [device(level, turn(a, d), b) for d in (1, 2, 3)]
    partners += [device(level, a, turn(b, d)) for d in (1, 2, 3)]
    partners += [device(lower, turn(a, d), b) for d in (0, 1, 2, 3)]
    partners += [device(upper, turn(a, d), b) for d in (0, 1, 2, 3)]
    for partner in partners:
        pl.semaphore_signal(barrier, inc=1, device_id=partner, device_id_type=MESH)

    shard_at = (core * 16 + b * 4 + a) * SHARD
    shard = pl.ds(shard_at, SHARD)

    def group(at_core, at_b):
        return pl.ds((at_core * 16 + at_b * 4) * SHARD, GROUP)

    def half(at_core):
        return pl.ds(at_core * HALF, HALF)

    def recv(panel, part, which):
        return recv_sem.at[(panel * PARTS + part) * 5 + which]

    def sent(panel, part, which):
        return send_sem.at[(panel * PARTS + part) * 3 + which]

    def spread(source, panel, part, target, turns):
        for d in turns:
            pltpu.make_async_remote_copy(
                src_ref=source,
                dst_ref=panels[panel][part].at[shard],
                send_sem=sent(panel, part, 0),
                recv_sem=recv(panel, part, 0),
                device_id=device(target, turn(a, d), b),
                device_id_type=MESH,
            ).start()

    def wait_bytes(ref, sem):
        pltpu.make_async_copy(ref, ref, sem).wait()

    def to_sibling(panel, part, which):
        ref = panels[panel][part].at[which]
        pltpu.make_async_remote_copy(
            src_ref=ref,
            dst_ref=ref,
            send_sem=sent(panel, part, 2),
            recv_sem=recv(panel, part, 4),
            device_id=sibling,
            device_id_type=MESH,
        ).start()

    def relay(panel, part):
        ref = panels[panel][part]
        mine = ref.at[group(core, b)]
        if panel == OWN:
            wait_bytes(ref.at[pl.ds(0, 3 * SHARD)], recv(panel, part, 0))
        else:
            wait_bytes(mine, recv(panel, part, 0))
        for d in (2, 1, 3):
            pltpu.make_async_remote_copy(
                src_ref=mine,
                dst_ref=mine,
                send_sem=sent(panel, part, 1),
                recv_sem=recv(panel, part, d),
                device_id=device(level, a, turn(b, d)),
                device_id_type=MESH,
            ).start()
        to_sibling(panel, part, group(core, b))

    def share(panel, part):
        for d in (1, 3, 2):
            theirs = group(core, turn(b, 4 - d))
            wait_bytes(panels[panel][part].at[theirs], recv(panel, part, d))
            to_sibling(panel, part, theirs)

    def complete(panel, part):
        wait_bytes(panels[panel][part].at[half(1 - core)], recv(panel, part, 4))

    def drain(panel, part, shards):
        ref = panels[panel][part]
        wait_bytes(ref.at[pl.ds(0, shards * SHARD)], sent(panel, part, 0))

    def drain_rest(panel, part):
        ref = panels[panel][part]
        wait_bytes(ref.at[pl.ds(0, 3 * GROUP)], sent(panel, part, 1))
        wait_bytes(ref.at[pl.ds(0, 4 * GROUP)], sent(panel, part, 2))

    loads[0].wait()
    for part in range(PARTS):
        for j in range(SHARD):
            rows = [
                x_vmem[PARTS * j + q].astype(F32)[part * WIDTH : (part + 1) * WIDTH]
                for q in range(PARTS)
            ]
            panels[OWN][part][shard_at + j] = jnp.concatenate(rows, axis=0).astype(BF16)

    pl.semaphore_wait(barrier, len(partners))
    for part in range(PARTS):
        mine = panels[OWN][part].at[shard]
        spread(mine, OWN, part, level, (2, 1, 3))
        spread(mine, ABOVE, part, lower, (2, 1, 3, 0))

    row_group = lax.broadcasted_iota(jnp.int32, (ROWS, TILE), 0) // WIDTH
    for q in range(PARTS + 1):
        masks[q] = jnp.where(row_group == q, 1.0, 0.0).astype(BF16)

    def index_row(i, carry):
        for band in range(3):
            count = counts[0, i, band]
            if band == ABOVE:
                count = jnp.where(level == LEVELS - 1, 0, count)
            for k in range(SLOTS):
                col = cols[0, i, band, k]
                owner, j = lax.shift_right_logical(col, 4), lax.bitwise_and(col, 15)
                oz = lax.shift_right_logical(owner, 3)
                oy = lax.bitwise_and(lax.shift_right_logical(owner, 1), 3)
                even = lax.bitwise_and(owner, 1) == 0
                pos = jnp.where(even, oz * 4 + oy, 16 + oy * 4 + oz)
                place[band, i * SLOTS + k] = pos * SHARD + j // PARTS
                pick[band, i * SLOTS + k] = jnp.where(k < count, lax.rem(j, PARTS), PARTS)
        return carry

    lax.fori_loop(0, ROWS, index_row, 0)

    loads[4].wait()

    def split_row(i, carry):
        whole = inv[i]
        high = whole.astype(BF16)
        inv_split[i, :, :TILE] = high
        inv_split[i, :, TILE:] = (whole - high.astype(F32)).astype(BF16)
        return carry

    lax.fori_loop(0, ROWS, split_row, 0)

    def band_term(band, tiles, part, i):
        panel = panels[band][part]
        pieces = [
            panel[place[band, i * SLOTS + k]] * masks[pick[band, i * SLOTS + k]]
            for k in range(SLOTS)
        ]
        left = jnp.concatenate(pieces, axis=1)
        right = tiles[i].reshape(SLOTS * TILE, TILE)
        return jnp.dot(left, right, preferred_element_type=F32)

    def solve(resid, i):
        high = resid.astype(BF16).astype(F32)
        both = jnp.concatenate([high, resid - high], axis=0).astype(BF16)
        four = jnp.dot(both, inv_split[i], preferred_element_type=F32)
        two = four[:, :TILE] + four[:, TILE:]
        return two[:WIDTH] + two[WIDTH:]

    STEP = 4

    def finish(part, resid_of):
        def rows(n, carry):
            done = []
            for m in range(STEP):
                i = n * STEP + m
                result = solve(resid_of(i), i)
                results[part][i] = result
                done.append(result)
            for m in range(STEP // PARTS):
                tile = jnp.concatenate(done[m * PARTS : (m + 1) * PARTS], axis=0)
                outgoing[part][n * (STEP // PARTS) + m] = tile.astype(BF16)
            return carry

        lax.fori_loop(0, ROWS // STEP, rows, 0)

        @pl.when(level < LEVELS - 1)
        def _():
            spread(outgoing[part], DOWN, part, upper, (2, 1, 3, 0))

        store(part).start()

    def store(part):
        return pltpu.make_async_copy(
            results[part],
            out_hbm.at[0, :, pl.ds(part * WIDTH, WIDTH), :],
            out_sem.at[part],
        )

    def base_rows(part):
        def rows(n, carry):
            for m in range(STEP):
                i = n * STEP + m
                total = band_term(OWN, level_t, part, i) + band_term(ABOVE, up, part, i)
                rhs = rhs_vmem[i, part * WIDTH : (part + 1) * WIDTH, :]
                bases[part][i] = rhs - fold(total)
            return carry

        lax.fori_loop(0, ROWS // STEP, rows, 0)

    relay(OWN, 0)
    relay(ABOVE, 0)
    for n in (1, 2, 3):
        loads[n].wait()
    for part in range(PARTS):
        if part + 1 < PARTS:
            relay(OWN, part + 1)
            relay(ABOVE, part + 1)
        share(OWN, part)
        share(ABOVE, part)
        complete(OWN, part)
        complete(ABOVE, part)
        base_rows(part)

        @pl.when(level == 0)
        def _():
            finish(part, lambda i: bases[part][i])

    loads[5].wait()

    @pl.when(level > 0)
    def _():
        relay(DOWN, 0)
        for part in range(PARTS):
            if part + 1 < PARTS:
                relay(DOWN, part + 1)
            share(DOWN, part)
            complete(DOWN, part)
            finish(part, lambda i: bases[part][i] - fold(band_term(DOWN, down, part, i)))

    for part in range(PARTS):
        drain(OWN, part, 3)
        drain(ABOVE, part, 4)
        drain_rest(OWN, part)
        drain_rest(ABOVE, part)

        @pl.when(level < LEVELS - 1)
        def _():
            drain(DOWN, part, 4)

        @pl.when(level > 0)
        def _():
            drain_rest(DOWN, part)

        store(part).wait()


def shards(x_old, rhs, down_tiles, level_tiles, up_tiles, inverses, tile_cols, tile_counts):
    in_hbm = pl.BlockSpec(memory_space=pltpu.HBM)
    in_smem = pl.BlockSpec(memory_space=pltpu.SMEM)
    panel = pltpu.VMEM((32 * SHARD, ROWS, TILE), BF16)
    part = pltpu.VMEM((ROWS, WIDTH, TILE), F32)
    return pl.pallas_call(
        sweep,
        out_shape=jax.ShapeDtypeStruct(rhs.shape, F32),
        in_specs=[in_hbm] * 6 + [in_smem] * 2,
        out_specs=in_hbm,
        scratch_shapes=[panel] * (3 * PARTS)
        + [pltpu.VMEM((SHARD, ROWS, TILE), BF16)] * PARTS
        + [part] * (2 * PARTS)
        + [
            pltpu.VMEM((ROWS, ROWS, TILE), BF16),
            pltpu.VMEM((ROWS, ROWS, TILE), F32),
            pltpu.VMEM((ROWS, SLOTS, TILE, TILE), BF16),
            pltpu.VMEM((ROWS, SLOTS, TILE, TILE), BF16),
            pltpu.VMEM((ROWS, SLOTS, TILE, TILE), BF16),
            pltpu.VMEM((ROWS, TILE, TILE), F32),
            pltpu.VMEM((ROWS, TILE, 2 * TILE), BF16),
            pltpu.VMEM((PARTS + 1, ROWS, TILE), BF16),
            pltpu.SMEM((3, ROWS * SLOTS), jnp.int32),
            pltpu.SMEM((3, ROWS * SLOTS), jnp.int32),
            pltpu.SemaphoreType.DMA((6,)),
            pltpu.SemaphoreType.DMA((PARTS,)),
            pltpu.SemaphoreType.DMA((3 * PARTS * 3,)),
            pltpu.SemaphoreType.DMA((3 * PARTS * 5,)),
        ],
        compiler_params=pltpu.CompilerParams(
            collective_id=0, has_side_effects=True, vmem_limit_bytes=60 * 1024 * 1024
        ),
        name="sweep",
    )(x_old, rhs, down_tiles, level_tiles, up_tiles, inverses, tile_cols, tile_counts)


def solution(mesh):
    return jax.shard_map(
        shards,
        mesh=mesh,
        in_specs=(
            P("level", "grp", None, None),
            P("level", "grp", None, None),
            P("level", "grp", None, None, None),
            P("level", "grp", None, None, None),
            P("level", "grp", None, None, None),
            P("level", "grp", None, None),
            P("level", "grp", None, None),
            P("level", "grp", None),
        ),
        out_specs=P("level", "grp", None, None),
        check_vma=False,
    )
```

```python
import jax
import jax.numpy as jnp
from jax import lax
from jax.experimental import pallas as pl
from jax.experimental.pallas import tpu as pltpu
from jax.sharding import PartitionSpec as P

MESH = pl.DeviceIdType.MESH
ROWS = 16
SLOTS = 6
TILE = 128
LEVELS = 4
PARTS = 4
WIDTH = ROWS // PARTS
SHARD = ROWS // PARTS
GROUP = 4 * SHARD
HALF = 16 * SHARD
TURNS = 2
SUBS = PARTS // TURNS
STEP = 16
OWN, ABOVE, DOWN = 1, 2, 0
F32, BF16 = jnp.float32, jnp.bfloat16


def fold(total):
    while total.shape[0] > WIDTH:
        half = total.shape[0] // 2
        total = total[:half] + total[half:]
    return total


def sweep(
    x_hbm, rhs_hbm, down_hbm, level_hbm, up_hbm, inv_hbm, cols, counts, out_hbm,
    panel_down, panel_own, panel_above, work, work_above, outgoing, results, bases, resid,
    x_vmem, rhs_vmem, down, level_t, up, inv, inv_split, masks, place, pick,
    load_sem, out_sem, send_sem, recv_sem,
):
    panels = {DOWN: panel_down, OWN: panel_own, ABOVE: panel_above}
    level = lax.axis_index("level")
    grp = lax.axis_index("grp")
    core = lax.rem(grp, 2)
    y = lax.rem(lax.div(grp, 2), 4)
    z = lax.div(grp, 8)
    first = core == 0
    a = jnp.where(first, y, z)
    b = jnp.where(first, z, y)
    lower = lax.rem(level + LEVELS - 1, LEVELS)
    upper = lax.rem(level + 1, LEVELS)

    def device(at_level, at_a, at_b):
        at_y = jnp.where(first, at_a, at_b)
        at_z = jnp.where(first, at_b, at_a)
        return (at_level, at_z * 8 + at_y * 2 + core)

    sibling = (level, z * 8 + y * 2 + 1 - core)

    def turn(value, by):
        return lax.rem(value + by, 4)

    loads = [
        (x_hbm.at[0], x_vmem),
        (level_hbm.at[0], level_t),
        (up_hbm.at[0], up),
        (rhs_hbm.at[0, :, pl.ds(0, 8), :], rhs_vmem.at[0]),
        (rhs_hbm.at[0, :, pl.ds(8, 8), :], rhs_vmem.at[1]),
        (inv_hbm.at[0], inv),
        (down_hbm.at[0], down),
    ]
    loads = [pltpu.make_async_copy(src, dst, load_sem.at[n]) for n, (src, dst) in enumerate(loads)]
    for load in loads:
        load.start()

    barrier = pltpu.get_barrier_semaphore()
    partners = [sibling]
    partners += [device(level, turn(a, d), b) for d in (1, 2, 3)]
    partners += [device(level, a, turn(b, d)) for d in (1, 2, 3)]
    partners += [device(lower, turn(a, d), b) for d in (0, 1, 2, 3)]
    partners += [device(upper, turn(a, d), b) for d in (0, 1, 2, 3)]
    for partner in partners:
        pl.semaphore_signal(barrier, inc=1, device_id=partner, device_id_type=MESH)

    shard_at = (core * 16 + b * 4 + a) * SHARD
    shard = pl.ds(shard_at, SHARD)

    def group(at_core, at_b):
        return pl.ds((at_core * 16 + at_b * 4) * SHARD, GROUP)

    def half(at_core):
        return pl.ds(at_core * HALF, HALF)

    def recv(panel, part, which):
        return recv_sem.at[(panel * PARTS + part) * 5 + which]

    def sent(panel, part, which):
        return send_sem.at[(panel * PARTS + part) * 3 + which]

    def spread(source, panel, part, target, turns):
        for d in turns:
            pltpu.make_async_remote_copy(
                src_ref=source,
                dst_ref=panels[panel].at[part].at[shard],
                send_sem=sent(panel, part, 0),
                recv_sem=recv(panel, part, 0),
                device_id=device(target, turn(a, d), b),
                device_id_type=MESH,
            ).start()

    def wait_bytes(ref, sem):
        pltpu.make_async_copy(ref, ref, sem).wait()

    def to_sibling(panel, part, which):
        ref = panels[panel].at[part].at[which]
        pltpu.make_async_remote_copy(
            src_ref=ref,
            dst_ref=ref,
            send_sem=sent(panel, part, 2),
            recv_sem=recv(panel, part, 4),
            device_id=sibling,
            device_id_type=MESH,
        ).start()

    def relay(panel, part):
        ref = panels[panel].at[part]
        mine = ref.at[group(core, b)]
        if panel == OWN:
            wait_bytes(ref.at[pl.ds(0, 3 * SHARD)], recv(panel, part, 0))
        else:
            wait_bytes(mine, recv(panel, part, 0))
        for d in (2, 1, 3):
            pltpu.make_async_remote_copy(
                src_ref=mine,
                dst_ref=mine,
                send_sem=sent(panel, part, 1),
                recv_sem=recv(panel, part, d),
                device_id=device(level, a, turn(b, d)),
                device_id_type=MESH,
            ).start()
        to_sibling(panel, part, group(core, b))

    def share(panel, part):
        for d in (1, 3, 2):
            theirs = group(core, turn(b, 4 - d))
            wait_bytes(panels[panel].at[part].at[theirs], recv(panel, part, d))
            to_sibling(panel, part, theirs)

    def complete(panel, part):
        wait_bytes(panels[panel].at[part].at[half(1 - core)], recv(panel, part, 4))

    def drain(panel, part, shards):
        ref = panels[panel].at[part]
        wait_bytes(ref.at[pl.ds(0, shards * SHARD)], sent(panel, part, 0))

    def drain_rest(panel, part):
        ref = panels[panel].at[part]
        wait_bytes(ref.at[pl.ds(0, 3 * GROUP)], sent(panel, part, 1))
        wait_bytes(ref.at[pl.ds(0, 4 * GROUP)], sent(panel, part, 2))

    loads[0].wait()
    for part in range(PARTS):
        for j in range(SHARD):
            rows = [
                x_vmem[PARTS * j + q].astype(F32)[part * WIDTH : (part + 1) * WIDTH]
                for q in range(PARTS)
            ]
            panels[OWN][part, shard_at + j] = jnp.concatenate(rows, axis=0).astype(BF16)

    pl.semaphore_wait(barrier, len(partners))
    for part in range(PARTS):
        mine = panels[OWN].at[part, shard]
        spread(mine, OWN, part, level, (2, 1, 3))
        spread(mine, ABOVE, part, lower, (2, 1, 3, 0))

    row_group = lax.broadcasted_iota(jnp.int32, (ROWS, TILE), 0) // WIDTH
    for q in range(PARTS + 1):
        masks[q] = jnp.where(row_group == q, 1.0, 0.0).astype(BF16)

    def index_row(i, carry):
        for band in range(3):
            count = counts[band, 0, i]
            if band == ABOVE:
                count = jnp.where(level == LEVELS - 1, 0, count)
            for k in range(SLOTS):
                col = cols[band, k, 0, i]
                owner, j = lax.shift_right_logical(col, 4), lax.bitwise_and(col, 15)
                oz = lax.shift_right_logical(owner, 3)
                oy = lax.bitwise_and(lax.shift_right_logical(owner, 1), 3)
                even = lax.bitwise_and(owner, 1) == 0
                pos = jnp.where(even, oz * 4 + oy, 16 + oy * 4 + oz)
                place[band, i * SLOTS + k] = pos * SHARD + j // PARTS
                pick[band, i * SLOTS + k] = jnp.where(k < count, lax.rem(j, PARTS), PARTS)
        return carry

    lax.fori_loop(0, ROWS, index_row, 0)

    loads[5].wait()

    def split_row(i, carry):
        whole = inv[i]
        high = whole.astype(BF16)
        inv_split[i, :, :TILE] = high
        inv_split[i, :, TILE:] = (whole - high.astype(F32)).astype(BF16)
        return carry

    lax.fori_loop(0, ROWS, split_row, 0)

    def band_term(band, tiles, blocks, i):
        pieces = [
            blocks[place[band, i * SLOTS + k]] * masks[pick[band, i * SLOTS + k]]
            for k in range(SLOTS)
        ]
        left = jnp.concatenate(pieces, axis=1)
        right = tiles[i].reshape(SLOTS * TILE, TILE)
        return jnp.dot(left, right, preferred_element_type=F32)

    def solve(rest, i):
        high = rest.astype(BF16).astype(F32)
        both = jnp.concatenate([high, rest - high], axis=0).astype(BF16)
        four = jnp.dot(both, inv_split[i], preferred_element_type=F32)
        two = four[:, :TILE] + four[:, TILE:]
        return two[:WIDTH] + two[WIDTH:]

    def all_rows(step):
        if STEP == ROWS:
            step(0)
        else:
            lax.fori_loop(0, ROWS // STEP, lambda n, carry: (step(n), carry)[1], 0)

    def base_rows(turn_, sub, part):
        def step(n):
            for m in range(STEP):
                i = n * STEP + m
                total = band_term(OWN, level_t, work, i) + band_term(ABOVE, up, work_above, i)
                rhs = rhs_vmem[turn_, i, sub * WIDTH : (sub + 1) * WIDTH, :]
                bases[part, i] = rhs - fold(total)

        all_rows(step)

    def down_rows(part):
        def step(n):
            for m in range(STEP):
                i = n * STEP + m
                resid[i] = bases[part, i] - fold(band_term(DOWN, down, work, i))

        all_rows(step)

    def finish(turn_, sub, part, rest_of):
        def step(n):
            done = []
            for m in range(STEP):
                i = n * STEP + m
                result = solve(rest_of(i), i)
                results[turn_, i, sub * WIDTH : (sub + 1) * WIDTH, :] = result
                done.append(result)
            for m in range(STEP // PARTS):
                tile = jnp.concatenate(done[m * PARTS : (m + 1) * PARTS], axis=0)
                outgoing[part, n * (STEP // PARTS) + m] = tile.astype(BF16)

        all_rows(step)

        @pl.when(level < LEVELS - 1)
        def _():
            spread(outgoing.at[part], DOWN, part, upper, (2, 1, 3, 0))

    def store(turn_):
        return pltpu.make_async_copy(
            results.at[turn_], out_hbm.at[0, :, pl.ds(turn_ * 8, 8), :], out_sem.at[turn_]
        )

    relay(OWN, 0)
    relay(ABOVE, 0)
    for n in (1, 2, 3, 4):
        loads[n].wait()

    def base_turn(turn_, carry):
        for sub in range(SUBS):
            part = turn_ * SUBS + sub

            @pl.when(part + 1 < PARTS)
            def _():
                relay(OWN, part + 1)
                relay(ABOVE, part + 1)

            share(OWN, part)
            share(ABOVE, part)
            complete(OWN, part)
            work[...] = panel_own[part]
            complete(ABOVE, part)
            work_above[...] = panel_above[part]
            base_rows(turn_, sub, part)

            @pl.when(level == 0)
            def _():
                finish(turn_, sub, part, lambda i: bases[part, i])

        @pl.when(level == 0)
        def _():
            store(turn_).start()

        return carry

    lax.fori_loop(0, TURNS, base_turn, 0)
    loads[6].wait()

    @pl.when(level > 0)
    def _():
        relay(DOWN, 0)

        def down_turn(turn_, carry):
            for sub in range(SUBS):
                part = turn_ * SUBS + sub

                @pl.when(part + 1 < PARTS)
                def _():
                    relay(DOWN, part + 1)

                share(DOWN, part)
                complete(DOWN, part)
                work[...] = panel_down[part]
                down_rows(part)
                finish(turn_, sub, part, lambda i: resid[i])

            store(turn_).start()
            return carry

        lax.fori_loop(0, TURNS, down_turn, 0)

    for turn_ in range(TURNS):
        store(turn_).wait()
    for part in range(PARTS):
        drain(OWN, part, 3)
        drain(ABOVE, part, 4)
        drain_rest(OWN, part)
        drain_rest(ABOVE, part)

        @pl.when(level < LEVELS - 1)
        def _():
            drain(DOWN, part, 4)

        @pl.when(level > 0)
        def _():
            drain_rest(DOWN, part)


def shards(x_old, rhs, down_tiles, level_tiles, up_tiles, inverses, tile_cols, tile_counts):
    cols = tile_cols.transpose(2, 3, 0, 1)
    counts = tile_counts.transpose(2, 0, 1)
    in_hbm = pl.BlockSpec(memory_space=pltpu.HBM)
    in_smem = pl.BlockSpec(memory_space=pltpu.SMEM)
    panel = pltpu.VMEM((PARTS, 32 * SHARD, ROWS, TILE), BF16)
    return pl.pallas_call(
        sweep,
        out_shape=jax.ShapeDtypeStruct(rhs.shape, F32),
        in_specs=[in_hbm] * 6 + [in_smem] * 2,
        out_specs=in_hbm,
        scratch_shapes=[panel] * 3
        + [
            pltpu.VMEM((32 * SHARD, ROWS, TILE), BF16),
            pltpu.VMEM((32 * SHARD, ROWS, TILE), BF16),
            pltpu.VMEM((PARTS, SHARD, ROWS, TILE), BF16),
            pltpu.VMEM((TURNS, ROWS, 8, TILE), F32),
            pltpu.VMEM((PARTS, ROWS, WIDTH, TILE), F32),
            pltpu.VMEM((ROWS, WIDTH, TILE), F32),
            pltpu.VMEM((ROWS, ROWS, TILE), BF16),
            pltpu.VMEM((TURNS, ROWS, 8, TILE), F32),
            pltpu.VMEM((ROWS, SLOTS, TILE, TILE), BF16),
            pltpu.VMEM((ROWS, SLOTS, TILE, TILE), BF16),
            pltpu.VMEM((ROWS, SLOTS, TILE, TILE), BF16),
            pltpu.VMEM((ROWS, TILE, TILE), F32),
            pltpu.VMEM((ROWS, TILE, 2 * TILE), BF16),
            pltpu.VMEM((PARTS + 1, ROWS, TILE), BF16),
            pltpu.SMEM((3, ROWS * SLOTS), jnp.int32),
            pltpu.SMEM((3, ROWS * SLOTS), jnp.int32),
            pltpu.SemaphoreType.DMA((7,)),
            pltpu.SemaphoreType.DMA((TURNS,)),
            pltpu.SemaphoreType.DMA((3 * PARTS * 3,)),
            pltpu.SemaphoreType.DMA((3 * PARTS * 5,)),
        ],
        compiler_params=pltpu.CompilerParams(
            collective_id=0, has_side_effects=True, vmem_limit_bytes=60 * 1024 * 1024
        ),
        name="sweep",
    )(x_old, rhs, down_tiles, level_tiles, up_tiles, inverses, cols, counts)


def solution(mesh):
    return jax.shard_map(
        shards,
        mesh=mesh,
        in_specs=(
            P("level", "grp", None, None),
            P("level", "grp", None, None),
            P("level", "grp", None, None, None),
            P("level", "grp", None, None, None),
            P("level", "grp", None, None, None),
            P("level", "grp", None, None),
            P("level", "grp", None, None),
            P("level", "grp", None),
        ),
        out_specs=P("level", "grp", None, None),
        check_vma=False,
    )
```

```python
import jax
import jax.numpy as jnp
from jax import lax
from jax.experimental import pallas as pl
from jax.experimental.pallas import tpu as pltpu
from jax.sharding import PartitionSpec as P

MESH = pl.DeviceIdType.MESH
ROWS = 16
SLOTS = 6
TILE = 128
LEVELS = 4
PARTS = 4
WIDTH = ROWS // PARTS
SHARD = ROWS // PARTS
GROUP = 4 * SHARD
HALF = 16 * SHARD
TURNS = 2
SUBS = PARTS // TURNS
STEP = 16
OWN, ABOVE, DOWN = 1, 2, 0
AHEAD = 2
F32, BF16 = jnp.float32, jnp.bfloat16


def fold(total):
    while total.shape[0] > WIDTH:
        half = total.shape[0] // 2
        total = total[:half] + total[half:]
    return total


def sweep(
    x_hbm, rhs_hbm, down_hbm, level_hbm, up_hbm, inv_hbm, cols, counts, out_hbm,
    panel_down, panel_own, panel_above, work, work_above, outgoing, results, bases, resid,
    x_vmem, rhs_vmem, down, level_t, up, inv, inv_split, masks, place, pick,
    load_sem, out_sem, send_sem, recv_sem,
):
    panels = {DOWN: panel_down, OWN: panel_own, ABOVE: panel_above}
    level = lax.axis_index("level")
    grp = lax.axis_index("grp")
    core = lax.rem(grp, 2)
    y = lax.rem(lax.div(grp, 2), 4)
    z = lax.div(grp, 8)
    def turn(value, by):
        return lax.rem(value + by, 4)

    lower = lax.rem(level + LEVELS - 1, LEVELS)
    upper = lax.rem(level + 1, LEVELS)
    along_y = {OWN: core == 0, ABOVE: core == 1, DOWN: core == 1}
    place_a = {panel: jnp.where(first, y, z) for panel, first in along_y.items()}
    place_b = {panel: jnp.where(first, z, y) for panel, first in along_y.items()}

    def device(panel, at_level, at_a, at_b):
        at_y = jnp.where(along_y[panel], at_a, at_b)
        at_z = jnp.where(along_y[panel], at_b, at_a)
        return (at_level, at_z * 8 + at_y * 2 + core)

    def around(panel, at_level, by_a, by_b):
        return device(panel, at_level, turn(place_a[panel], by_a), turn(place_b[panel], by_b))

    sibling = (level, z * 8 + y * 2 + 1 - core)

    loads = [
        (x_hbm.at[0], x_vmem),
        (level_hbm.at[0], level_t),
        (up_hbm.at[0], up),
        (rhs_hbm.at[0, :, pl.ds(0, 8), :], rhs_vmem.at[0]),
        (rhs_hbm.at[0, :, pl.ds(8, 8), :], rhs_vmem.at[1]),
        (inv_hbm.at[0], inv),
        (down_hbm.at[0], down),
    ]
    loads = [pltpu.make_async_copy(src, dst, load_sem.at[n]) for n, (src, dst) in enumerate(loads)]
    for load in loads:
        load.start()

    barrier = pltpu.get_barrier_semaphore()
    partners = [sibling]
    partners += [around(OWN, level, d, 0) for d in (1, 2, 3)]
    partners += [around(OWN, level, 0, d) for d in (1, 2, 3)]
    partners += [around(ABOVE, lower, d, 0) for d in (0, 1, 2, 3)]
    partners += [around(DOWN, upper, d, 0) for d in (0, 1, 2, 3)]
    for partner in partners:
        pl.semaphore_signal(barrier, inc=1, device_id=partner, device_id_type=MESH)

    def shard_at(panel, by_a):
        return (core * 16 + place_b[panel] * 4 + turn(place_a[panel], by_a)) * SHARD

    def shard(panel, by_a=0):
        return pl.ds(shard_at(panel, by_a), SHARD)

    def group(panel, by_b):
        return pl.ds((core * 16 + turn(place_b[panel], by_b) * 4) * SHARD, GROUP)

    def half(at_core):
        return pl.ds(at_core * HALF, HALF)

    def recv(panel, part, which):
        return recv_sem.at[(panel * PARTS + part) * 8 + which]

    def sent(panel, part, which):
        return send_sem.at[(panel * PARTS + part) * 4 + which]

    def spread(source, panel, part, target, turns):
        for d in turns:
            pltpu.make_async_remote_copy(
                src_ref=source,
                dst_ref=panels[panel].at[part, shard(panel)],
                send_sem=sent(panel, part, 0),
                recv_sem=recv(panel, part, d),
                device_id=around(panel, target, d, 0),
                device_id_type=MESH,
            ).start()

    def wait_bytes(ref, sem):
        pltpu.make_async_copy(ref, ref, sem).wait()

    def to_sibling(panel, part, which):
        ref = panels[panel].at[part].at[which]
        pltpu.make_async_remote_copy(
            src_ref=ref,
            dst_ref=ref,
            send_sem=sent(panel, part, 2),
            recv_sem=recv(panel, part, 4),
            device_id=sibling,
            device_id_type=MESH,
        ).start()

    def send_on(panel, part, by_a):
        ref = panels[panel].at[part, shard(panel, by_a)]
        for d in (2, 1, 3):
            pltpu.make_async_remote_copy(
                src_ref=ref,
                dst_ref=ref,
                send_sem=sent(panel, part, 1),
                recv_sem=recv(panel, part, 4 + d),
                device_id=around(panel, level, 0, d),
                device_id_type=MESH,
            ).start()

    def relay(panel, part):
        for d in (1, 3, 2) if panel == OWN else (0, 1, 3, 2):
            wait_bytes(panels[panel].at[part, shard(panel, 4 - d)], recv(panel, part, d))
            send_on(panel, part, 4 - d)
        to_sibling(panel, part, group(panel, 0))

    def share(panel, part):
        for d in (1, 3, 2):
            theirs = group(panel, 4 - d)
            wait_bytes(panels[panel].at[part, theirs], recv(panel, part, 4 + d))
            to_sibling(panel, part, theirs)

    def complete(panel, part):
        wait_bytes(panels[panel].at[part].at[half(1 - core)], recv(panel, part, 4))

    def drain(panel, part, shards):
        ref = panels[panel].at[part]
        wait_bytes(ref.at[pl.ds(0, shards * SHARD)], sent(panel, part, 0))

    def drain_rest(panel, part):
        ref = panels[panel].at[part]
        wait_bytes(ref.at[pl.ds(0, 3 * GROUP)], sent(panel, part, 1))
        wait_bytes(ref.at[pl.ds(0, 4 * GROUP)], sent(panel, part, 2))

    loads[0].wait()
    for part in range(PARTS):
        for j in range(SHARD):
            rows = [
                x_vmem[PARTS * j + q].astype(F32)[part * WIDTH : (part + 1) * WIDTH]
                for q in range(PARTS)
            ]
            panels[OWN][part, shard_at(OWN, 0) + j] = jnp.concatenate(rows, axis=0).astype(BF16)

    pl.semaphore_wait(barrier, len(partners))
    for part in range(PARTS):
        mine = panels[OWN].at[part, shard(OWN)]
        spread(mine, OWN, part, level, (2, 1, 3))

        @pl.when(level > 0)
        def _():
            spread(mine, ABOVE, part, lower, (2, 1, 3, 0))

        send_on(OWN, part, 0)

    row_group = lax.broadcasted_iota(jnp.int32, (ROWS, TILE), 0) // WIDTH
    for q in range(PARTS + 1):
        masks[q] = jnp.where(row_group == q, 1.0, 0.0).astype(BF16)

    def index_row(i, carry):
        for band in range(3):
            count = counts[band, 0, i]
            if band == ABOVE:
                count = jnp.where(level == LEVELS - 1, 0, count)
            for k in range(SLOTS):
                col = cols[band, k, 0, i]
                owner, j = lax.shift_right_logical(col, 4), lax.bitwise_and(col, 15)
                oz = lax.shift_right_logical(owner, 3)
                oy = lax.bitwise_and(lax.shift_right_logical(owner, 1), 3)
                even = lax.bitwise_and(owner, 1) == 0
                pos = jnp.where(even, 0, 16) + jnp.where(
                    even == (band == OWN), oz * 4 + oy, oy * 4 + oz
                )
                place[band, i * SLOTS + k] = pos * SHARD + j // PARTS
                pick[band, i * SLOTS + k] = jnp.where(k < count, lax.rem(j, PARTS), PARTS)
        return carry

    lax.fori_loop(0, ROWS, index_row, 0)

    loads[5].wait()

    def split_row(i, carry):
        whole = inv[i]
        high = whole.astype(BF16)
        inv_split[i, :, :TILE] = high
        inv_split[i, :, TILE:] = (whole - high.astype(F32)).astype(BF16)
        return carry

    lax.fori_loop(0, ROWS, split_row, 0)

    def band_term(band, tiles, blocks, i):
        pieces = [
            blocks[place[band, i * SLOTS + k]] * masks[pick[band, i * SLOTS + k]]
            for k in range(SLOTS)
        ]
        left = jnp.concatenate(pieces, axis=1)
        right = tiles[i].reshape(SLOTS * TILE, TILE)
        return jnp.dot(left, right, preferred_element_type=F32)

    def solve(rest, i):
        high = rest.astype(BF16).astype(F32)
        both = jnp.concatenate([high, rest - high], axis=0).astype(BF16)
        four = jnp.dot(both, inv_split[i], preferred_element_type=F32)
        two = four[:, :TILE] + four[:, TILE:]
        return two[:WIDTH] + two[WIDTH:]

    def all_rows(step):
        if STEP == ROWS:
            step(0)
        else:
            lax.fori_loop(0, ROWS // STEP, lambda n, carry: (step(n), carry)[1], 0)

    def base_rows(turn_, sub, part):
        def step(n):
            for m in range(STEP):
                i = n * STEP + m
                total = band_term(OWN, level_t, work, i) + band_term(ABOVE, up, work_above, i)
                rhs = rhs_vmem[turn_, i, sub * WIDTH : (sub + 1) * WIDTH, :]
                bases[part, i] = rhs - fold(total)

        all_rows(step)

    def down_rows(part):
        def step(n):
            for m in range(STEP):
                i = n * STEP + m
                resid[i] = bases[part, i] - fold(band_term(DOWN, down, work, i))

        all_rows(step)

    def finish(turn_, sub, part, rest_of):
        def step(n):
            done = []
            for m in range(STEP):
                i = n * STEP + m
                result = solve(rest_of(i), i)
                results[turn_, i, sub * WIDTH : (sub + 1) * WIDTH, :] = result
                done.append(result)
            for m in range(STEP // PARTS):
                tile = jnp.concatenate(done[m * PARTS : (m + 1) * PARTS], axis=0)
                outgoing[part, n * (STEP // PARTS) + m] = tile.astype(BF16)

        all_rows(step)

        @pl.when(level < LEVELS - 1)
        def _():
            spread(outgoing.at[part], DOWN, part, upper, (2, 1, 3, 0))

    def store(turn_):
        return pltpu.make_async_copy(
            results.at[turn_], out_hbm.at[0, :, pl.ds(turn_ * 8, 8), :], out_sem.at[turn_]
        )

    def relay_both(part):
        relay(OWN, part)

        @pl.when(level < LEVELS - 1)
        def _():
            relay(ABOVE, part)

    for part in range(AHEAD):
        relay_both(part)

    @pl.when(level == LEVELS - 1)
    def _():
        work_above[...] = jnp.zeros_like(work_above)

    for n in (1, 2, 3, 4):
        loads[n].wait()

    def base_turn(turn_, carry):
        for sub in range(SUBS):
            part = turn_ * SUBS + sub

            @pl.when(part + AHEAD < PARTS)
            def _():
                relay_both(part + AHEAD)

            share(OWN, part)

            @pl.when(level < LEVELS - 1)
            def _():
                share(ABOVE, part)

            complete(OWN, part)
            work[...] = panel_own[part]

            @pl.when(level < LEVELS - 1)
            def _():
                complete(ABOVE, part)
                work_above[...] = panel_above[part]

            base_rows(turn_, sub, part)

            @pl.when(level == 0)
            def _():
                finish(turn_, sub, part, lambda i: bases[part, i])

            @pl.when((level == 1) & (part > 0))
            def _():
                relay(DOWN, part - 1)

        @pl.when(level == 0)
        def _():
            store(turn_).start()

        return carry

    lax.fori_loop(0, TURNS, base_turn, 0)
    loads[6].wait()

    @pl.when(level > 0)
    def _():
        @pl.when(level > 1)
        def _():
            relay(DOWN, 0)

        def down_turn(turn_, carry):
            for sub in range(SUBS):
                part = turn_ * SUBS + sub

                @pl.when((part + 1 < PARTS) & ((level > 1) | (part + 2 == PARTS)))
                def _():
                    relay(DOWN, part + 1)

                share(DOWN, part)
                complete(DOWN, part)
                work[...] = panel_down[part]
                down_rows(part)
                finish(turn_, sub, part, lambda i: resid[i])

            store(turn_).start()
            return carry

        lax.fori_loop(0, TURNS, down_turn, 0)

    for turn_ in range(TURNS):
        store(turn_).wait()
    for part in range(PARTS):
        drain(OWN, part, 3)
        drain_rest(OWN, part)

        @pl.when(level < LEVELS - 1)
        def _():
            drain(DOWN, part, 4)
            drain_rest(ABOVE, part)

        @pl.when(level > 0)
        def _():
            drain(ABOVE, part, 4)
            drain_rest(DOWN, part)


def shards(x_old, rhs, down_tiles, level_tiles, up_tiles, inverses, tile_cols, tile_counts):
    cols = tile_cols.transpose(2, 3, 0, 1)
    counts = tile_counts.transpose(2, 0, 1)
    in_hbm = pl.BlockSpec(memory_space=pltpu.HBM)
    in_smem = pl.BlockSpec(memory_space=pltpu.SMEM)
    panel = pltpu.VMEM((PARTS, 32 * SHARD, ROWS, TILE), BF16)
    return pl.pallas_call(
        sweep,
        out_shape=jax.ShapeDtypeStruct(rhs.shape, F32),
        in_specs=[in_hbm] * 6 + [in_smem] * 2,
        out_specs=in_hbm,
        scratch_shapes=[panel] * 3
        + [
            pltpu.VMEM((32 * SHARD, ROWS, TILE), BF16),
            pltpu.VMEM((32 * SHARD, ROWS, TILE), BF16),
            pltpu.VMEM((PARTS, SHARD, ROWS, TILE), BF16),
            pltpu.VMEM((TURNS, ROWS, 8, TILE), F32),
            pltpu.VMEM((PARTS, ROWS, WIDTH, TILE), F32),
            pltpu.VMEM((ROWS, WIDTH, TILE), F32),
            pltpu.VMEM((ROWS, ROWS, TILE), BF16),
            pltpu.VMEM((TURNS, ROWS, 8, TILE), F32),
            pltpu.VMEM((ROWS, SLOTS, TILE, TILE), BF16),
            pltpu.VMEM((ROWS, SLOTS, TILE, TILE), BF16),
            pltpu.VMEM((ROWS, SLOTS, TILE, TILE), BF16),
            pltpu.VMEM((ROWS, TILE, TILE), F32),
            pltpu.VMEM((ROWS, TILE, 2 * TILE), BF16),
            pltpu.VMEM((PARTS + 1, ROWS, TILE), BF16),
            pltpu.SMEM((3, ROWS * SLOTS), jnp.int32),
            pltpu.SMEM((3, ROWS * SLOTS), jnp.int32),
            pltpu.SemaphoreType.DMA((7,)),
            pltpu.SemaphoreType.DMA((TURNS,)),
            pltpu.SemaphoreType.DMA((3 * PARTS * 4,)),
            pltpu.SemaphoreType.DMA((3 * PARTS * 8,)),
        ],
        compiler_params=pltpu.CompilerParams(
            collective_id=0, has_side_effects=True, vmem_limit_bytes=60 * 1024 * 1024
        ),
        name="sweep",
    )(x_old, rhs, down_tiles, level_tiles, up_tiles, inverses, cols, counts)


def solution(mesh):
    return jax.shard_map(
        shards,
        mesh=mesh,
        in_specs=(
            P("level", "grp", None, None),
            P("level", "grp", None, None),
            P("level", "grp", None, None, None),
            P("level", "grp", None, None, None),
            P("level", "grp", None, None, None),
            P("level", "grp", None, None),
            P("level", "grp", None, None),
            P("level", "grp", None),
        ),
        out_specs=P("level", "grp", None, None),
        check_vma=False,
    )
```

```python
import jax
import jax.numpy as jnp
from jax import lax
from jax.experimental import pallas as pl
from jax.experimental.pallas import tpu as pltpu
from jax.sharding import PartitionSpec as P

MESH = pl.DeviceIdType.MESH
ROWS = 16
SLOTS = 6
TILE = 128
LEVELS = 4
PARTS = 4
WIDTH = ROWS // PARTS
SHARD = ROWS // PARTS
GROUP = 4 * SHARD
HALF = 16 * SHARD
TURNS = 2
SUBS = PARTS // TURNS
STEP = 16
OWN, ABOVE, DOWN = 1, 2, 0
AHEAD = 2
DOWN_AHEAD = 2
LATE_AHEAD = 2
BETWEEN = 1
S2_ORDER = (2, 1, 3)
S1_ORDER = (2, 1, 3, 0)
BASE_FROM = 2
F32, BF16 = jnp.float32, jnp.bfloat16


def fold(total):
    while total.shape[0] > WIDTH:
        half = total.shape[0] // 2
        total = total[:half] + total[half:]
    return total


def sweep(
    x_hbm, rhs_hbm, down_hbm, level_hbm, up_hbm, inv_hbm, cols, counts, out_ref,
    panel_down, panel_own, panel_above, work, work_above, outgoing, results, bases, resid,
    x_vmem, rhs_vmem, down, level_t, up, inv, inv_split, masks, place, pick,
    load_sem, send_sem, recv_sem,
):
    panels = {DOWN: panel_down, OWN: panel_own, ABOVE: panel_above}
    level = lax.axis_index("level")
    grp = lax.axis_index("grp")
    core = lax.rem(grp, 2)
    y = lax.rem(lax.div(grp, 2), 4)
    z = lax.div(grp, 8)
    def turn(value, by):
        return lax.rem(value + by, 4)

    lower = lax.rem(level + LEVELS - 1, LEVELS)
    upper = lax.rem(level + 1, LEVELS)
    along_y = {OWN: core == 0, ABOVE: core == 1, DOWN: core == 1}
    place_a = {panel: jnp.where(first, y, z) for panel, first in along_y.items()}
    place_b = {panel: jnp.where(first, z, y) for panel, first in along_y.items()}

    def device(panel, at_level, at_a, at_b):
        at_y = jnp.where(along_y[panel], at_a, at_b)
        at_z = jnp.where(along_y[panel], at_b, at_a)
        return (at_level, at_z * 8 + at_y * 2 + core)

    def around(panel, at_level, by_a, by_b):
        return device(panel, at_level, turn(place_a[panel], by_a), turn(place_b[panel], by_b))

    sibling = (level, z * 8 + y * 2 + 1 - core)

    loads = [
        (x_hbm.at[0], x_vmem),
        (level_hbm.at[0], level_t),
        (up_hbm.at[0], up),
        (rhs_hbm.at[0, :, pl.ds(0, 8), :], rhs_vmem.at[0]),
        (rhs_hbm.at[0, :, pl.ds(8, 8), :], rhs_vmem.at[1]),
        (inv_hbm.at[0], inv),
        (down_hbm.at[0], down),
    ]
    loads = [pltpu.make_async_copy(src, dst, load_sem.at[n]) for n, (src, dst) in enumerate(loads)]
    for load in loads:
        load.start()

    barrier = pltpu.get_barrier_semaphore()
    partners = [sibling]
    partners += [around(OWN, level, d, 0) for d in (1, 2, 3)]
    partners += [around(OWN, level, 0, d) for d in (1, 2, 3)]
    partners += [around(ABOVE, lower, d, 0) for d in (0, 1, 2, 3)]
    partners += [around(DOWN, upper, d, 0) for d in (0, 1, 2, 3)]
    for partner in partners:
        pl.semaphore_signal(barrier, inc=1, device_id=partner, device_id_type=MESH)

    def shard_at(panel, by_a):
        return (core * 16 + place_b[panel] * 4 + turn(place_a[panel], by_a)) * SHARD

    def shard(panel, by_a=0):
        return pl.ds(shard_at(panel, by_a), SHARD)

    def group(panel, by_b):
        return pl.ds((core * 16 + turn(place_b[panel], by_b) * 4) * SHARD, GROUP)

    def half(at_core):
        return pl.ds(at_core * HALF, HALF)

    def recv(panel, part, which):
        return recv_sem.at[(panel * PARTS + part) * 8 + which]

    def sent(panel, part, which):
        return send_sem.at[(panel * PARTS + part) * 4 + which]

    def spread(source, panel, part, target, turns):
        for d in turns:
            pltpu.make_async_remote_copy(
                src_ref=source,
                dst_ref=panels[panel].at[part, shard(panel)],
                send_sem=sent(panel, part, 0),
                recv_sem=recv(panel, part, d),
                device_id=around(panel, target, d, 0),
                device_id_type=MESH,
            ).start()

    def wait_bytes(ref, sem):
        pltpu.make_async_copy(ref, ref, sem).wait()

    def to_sibling(panel, part, which):
        ref = panels[panel].at[part].at[which]
        pltpu.make_async_remote_copy(
            src_ref=ref,
            dst_ref=ref,
            send_sem=sent(panel, part, 2),
            recv_sem=recv(panel, part, 4),
            device_id=sibling,
            device_id_type=MESH,
        ).start()

    def send_on(panel, part, by_a):
        ref = panels[panel].at[part, shard(panel, by_a)]
        for d in S2_ORDER:
            pltpu.make_async_remote_copy(
                src_ref=ref,
                dst_ref=ref,
                send_sem=sent(panel, part, 1),
                recv_sem=recv(panel, part, 4 + d),
                device_id=around(panel, level, 0, d),
                device_id_type=MESH,
            ).start()

    def relay(panel, part):
        for d in (1, 3, 2) if panel == OWN else (0, 1, 3, 2):
            wait_bytes(panels[panel].at[part, shard(panel, 4 - d)], recv(panel, part, d))
            send_on(panel, part, 4 - d)
        to_sibling(panel, part, group(panel, 0))

    def share(panel, part):
        for d in (1, 3, 2):
            theirs = group(panel, 4 - d)
            wait_bytes(panels[panel].at[part, theirs], recv(panel, part, 4 + d))
            to_sibling(panel, part, theirs)

    def complete(panel, part):
        wait_bytes(panels[panel].at[part].at[half(1 - core)], recv(panel, part, 4))

    def drain(panel, part, shards):
        ref = panels[panel].at[part]
        wait_bytes(ref.at[pl.ds(0, shards * SHARD)], sent(panel, part, 0))

    def drain_rest(panel, part):
        ref = panels[panel].at[part]
        wait_bytes(ref.at[pl.ds(0, 3 * GROUP)], sent(panel, part, 1))
        wait_bytes(ref.at[pl.ds(0, 4 * GROUP)], sent(panel, part, 2))

    loads[0].wait()
    for part in range(PARTS):
        for j in range(SHARD):
            rows = [
                x_vmem[PARTS * j + q].astype(F32)[part * WIDTH : (part + 1) * WIDTH]
                for q in range(PARTS)
            ]
            panels[OWN][part, shard_at(OWN, 0) + j] = jnp.concatenate(rows, axis=0).astype(BF16)

    pl.semaphore_wait(barrier, len(partners))
    for part in range(PARTS):
        mine = panels[OWN].at[part, shard(OWN)]
        spread(mine, OWN, part, level, (2, 1, 3))

        @pl.when(level > 0)
        def _():
            spread(mine, ABOVE, part, lower, (2, 1, 3, 0))

        send_on(OWN, part, 0)

    row_group = lax.broadcasted_iota(jnp.int32, (ROWS, TILE), 0) // WIDTH
    for q in range(PARTS + 1):
        masks[q] = jnp.where(row_group == q, 1.0, 0.0).astype(BF16)

    def index_row(i, carry):
        for band in range(3):
            count = counts[band, 0, i]
            if band == ABOVE:
                count = jnp.where(level == LEVELS - 1, 0, count)
            for k in range(SLOTS):
                col = cols[band, k, 0, i]
                owner, j = lax.shift_right_logical(col, 4), lax.bitwise_and(col, 15)
                oz = lax.shift_right_logical(owner, 3)
                oy = lax.bitwise_and(lax.shift_right_logical(owner, 1), 3)
                even = lax.bitwise_and(owner, 1) == 0
                pos = jnp.where(even, 0, 16) + jnp.where(
                    even == (band == OWN), oz * 4 + oy, oy * 4 + oz
                )
                place[band, i * SLOTS + k] = pos * SHARD + j // PARTS
                pick[band, i * SLOTS + k] = jnp.where(k < count, lax.rem(j, PARTS), PARTS)
        return carry

    lax.fori_loop(0, ROWS, index_row, 0)

    loads[5].wait()

    def split_row(i, carry):
        whole = inv[i]
        high = whole.astype(BF16)
        inv_split[i, :, :TILE] = high
        inv_split[i, :, TILE:] = (whole - high.astype(F32)).astype(BF16)
        return carry

    lax.fori_loop(0, ROWS, split_row, 0)

    def band_term(band, tiles, blocks, i):
        pieces = [
            blocks[place[band, i * SLOTS + k]] * masks[pick[band, i * SLOTS + k]]
            for k in range(SLOTS)
        ]
        left = jnp.concatenate(pieces, axis=1)
        right = tiles[i].reshape(SLOTS * TILE, TILE)
        return jnp.dot(left, right, preferred_element_type=F32)

    def solve(rest, i):
        high = rest.astype(BF16).astype(F32)
        both = jnp.concatenate([high, rest - high], axis=0).astype(BF16)
        four = jnp.dot(both, inv_split[i], preferred_element_type=F32)
        two = four[:, :TILE] + four[:, TILE:]
        return two[:WIDTH] + two[WIDTH:]

    def all_rows(step):
        if STEP == ROWS:
            step(0)
        else:
            lax.fori_loop(0, ROWS // STEP, lambda n, carry: (step(n), carry)[1], 0)

    def base_rows(turn_, sub, part):
        def step(n):
            for m in range(STEP):
                i = n * STEP + m
                total = band_term(OWN, level_t, work, i) + band_term(ABOVE, up, work_above, i)
                rhs = rhs_vmem[turn_, i, sub * WIDTH : (sub + 1) * WIDTH, :]
                bases[part, i] = rhs - fold(total)

        all_rows(step)

    def down_rows(part):
        def step(n):
            for m in range(STEP):
                i = n * STEP + m
                resid[i] = bases[part, i] - fold(band_term(DOWN, down, work, i))

        all_rows(step)

    def finish(turn_, sub, part, rest_of):
        def step(n):
            done = []
            for m in range(STEP):
                i = n * STEP + m
                result = solve(rest_of(i), i)
                results[turn_, i, sub * WIDTH : (sub + 1) * WIDTH, :] = result
                done.append(result)
            for m in range(STEP // PARTS):
                tile = jnp.concatenate(done[m * PARTS : (m + 1) * PARTS], axis=0)
                outgoing[part, n * (STEP // PARTS) + m] = tile.astype(BF16)

        all_rows(step)

        @pl.when(level < LEVELS - 1)
        def _():
            spread(outgoing.at[part], DOWN, part, upper, S1_ORDER)

    def relay_both(part):
        relay(OWN, part)

        @pl.when(level < LEVELS - 1)
        def _():
            relay(ABOVE, part)

    def share_both(part):
        share(OWN, part)

        @pl.when(level < LEVELS - 1)
        def _():
            share(ABOVE, part)

    for part in range(AHEAD):
        relay_both(part)

    @pl.when(level == LEVELS - 1)
    def _():
        work_above[...] = jnp.zeros_like(work_above)

    for n in (1, 2, 3, 4):
        loads[n].wait()

    def base_turn(turn_, carry):
        for sub in range(SUBS):
            part = turn_ * SUBS + sub

            @pl.when(part + AHEAD < PARTS)
            def _():
                relay_both(part + AHEAD)

            @pl.when(part <= BASE_FROM)
            def _():
                share_both(part)

            @pl.when((part >= BASE_FROM) & (part + 1 < PARTS))
            def _():
                share_both(part + 1)

            complete(OWN, part)
            work[...] = panel_own[part]

            @pl.when(level < LEVELS - 1)
            def _():
                complete(ABOVE, part)
                work_above[...] = panel_above[part]

            base_rows(turn_, sub, part)

            @pl.when(level == 0)
            def _():
                finish(turn_, sub, part, lambda i: bases[part, i])

            @pl.when((level == 1) & (part >= BETWEEN))
            def _():
                relay(DOWN, part - BETWEEN)

        return carry

    lax.fori_loop(0, TURNS, base_turn, 0)
    loads[6].wait()

    @pl.when(level > 0)
    def _():
        @pl.when(level > 1)
        def _():
            for part in range(LATE_AHEAD):
                relay(DOWN, part)

        def down_turn(turn_, carry):
            for sub in range(SUBS):
                part = turn_ * SUBS + sub

                later = part + jnp.where(level > 1, LATE_AHEAD, DOWN_AHEAD)

                @pl.when((later < PARTS) & ((level > 1) | (later >= PARTS - BETWEEN)))
                def _():
                    relay(DOWN, later)

                share(DOWN, part)
                complete(DOWN, part)
                work[...] = panel_down[part]
                down_rows(part)
                finish(turn_, sub, part, lambda i: resid[i])

            return carry

        lax.fori_loop(0, TURNS, down_turn, 0)

    for turn_ in range(TURNS):
        out_ref[0, :, turn_ * 8 : (turn_ + 1) * 8, :] = results[turn_]
    for part in range(PARTS):
        drain(OWN, part, 3)
        drain_rest(OWN, part)

        @pl.when(level < LEVELS - 1)
        def _():
            drain(DOWN, part, 4)
            drain_rest(ABOVE, part)

        @pl.when(level > 0)
        def _():
            drain(ABOVE, part, 4)
            drain_rest(DOWN, part)


def shards(x_old, rhs, down_tiles, level_tiles, up_tiles, inverses, tile_cols, tile_counts):
    cols = tile_cols.transpose(2, 3, 0, 1)
    counts = tile_counts.transpose(2, 0, 1)
    in_hbm = pl.BlockSpec(memory_space=pltpu.HBM)
    in_smem = pl.BlockSpec(memory_space=pltpu.SMEM)
    panel = pltpu.VMEM((PARTS, 32 * SHARD, ROWS, TILE), BF16)
    return pl.pallas_call(
        sweep,
        out_shape=pltpu.VMEM(rhs.shape, F32),
        in_specs=[in_hbm] * 6 + [in_smem] * 2,
        out_specs=pl.BlockSpec(memory_space=pltpu.VMEM),
        scratch_shapes=[panel] * 3
        + [
            pltpu.VMEM((32 * SHARD, ROWS, TILE), BF16),
            pltpu.VMEM((32 * SHARD, ROWS, TILE), BF16),
            pltpu.VMEM((PARTS, SHARD, ROWS, TILE), BF16),
            pltpu.VMEM((TURNS, ROWS, 8, TILE), F32),
            pltpu.VMEM((PARTS, ROWS, WIDTH, TILE), F32),
            pltpu.VMEM((ROWS, WIDTH, TILE), F32),
            pltpu.VMEM((ROWS, ROWS, TILE), BF16),
            pltpu.VMEM((TURNS, ROWS, 8, TILE), F32),
            pltpu.VMEM((ROWS, SLOTS, TILE, TILE), BF16),
            pltpu.VMEM((ROWS, SLOTS, TILE, TILE), BF16),
            pltpu.VMEM((ROWS, SLOTS, TILE, TILE), BF16),
            pltpu.VMEM((ROWS, TILE, TILE), F32),
            pltpu.VMEM((ROWS, TILE, 2 * TILE), BF16),
            pltpu.VMEM((PARTS + 1, ROWS, TILE), BF16),
            pltpu.SMEM((3, ROWS * SLOTS), jnp.int32),
            pltpu.SMEM((3, ROWS * SLOTS), jnp.int32),
            pltpu.SemaphoreType.DMA((7,)),
            pltpu.SemaphoreType.DMA((3 * PARTS * 4,)),
            pltpu.SemaphoreType.DMA((3 * PARTS * 8,)),
        ],
        compiler_params=pltpu.CompilerParams(
            collective_id=0, has_side_effects=True, vmem_limit_bytes=60 * 1024 * 1024
        ),
        name="sweep",
    )(x_old, rhs, down_tiles, level_tiles, up_tiles, inverses, cols, counts)


def solution(mesh):
    return jax.shard_map(
        shards,
        mesh=mesh,
        in_specs=(
            P("level", "grp", None, None),
            P("level", "grp", None, None),
            P("level", "grp", None, None, None),
            P("level", "grp", None, None, None),
            P("level", "grp", None, None, None),
            P("level", "grp", None, None),
            P("level", "grp", None, None),
            P("level", "grp", None),
        ),
        out_specs=P("level", "grp", None, None),
        check_vma=False,
    )
```

```python
import jax
import jax.numpy as jnp
from jax import lax
from jax.experimental import pallas as pl
from jax.experimental.pallas import tpu as pltpu
from jax.sharding import PartitionSpec as P

MESH = pl.DeviceIdType.MESH
ROWS = 16
SLOTS = 6
TILE = 128
LEVELS = 4
PARTS = 4
WIDTH = ROWS // PARTS
SHARD = ROWS // PARTS
GROUP = 4 * SHARD
HALF = 16 * SHARD
TURNS = 2
SUBS = PARTS // TURNS
STEP = 16
OWN, ABOVE, DOWN = 1, 2, 0
AHEAD = 3
DOWN_AHEAD = 2
LATE_AHEAD = 2
BETWEEN = 1
S2_ORDER = (2, 1, 3)
S1_ORDER = (2, 1, 3, 0)
BASE_FROM = 1
F32, BF16 = jnp.float32, jnp.bfloat16


def fold(total):
    while total.shape[0] > WIDTH:
        half = total.shape[0] // 2
        total = total[:half] + total[half:]
    return total


def sweep(
    x_hbm, rhs_hbm, down_hbm, level_hbm, up_hbm, inv_hbm, cols, counts, out_ref,
    panel_down, panel_own, panel_above, work, work_above, outgoing, results, bases, resid,
    x_vmem, rhs_vmem, down, level_t, up, inv, inv_split, masks, place, pick,
    load_sem, send_sem, recv_sem,
):
    panels = {DOWN: panel_down, OWN: panel_own, ABOVE: panel_above}
    level = lax.axis_index("level")
    grp = lax.axis_index("grp")
    core = lax.rem(grp, 2)
    y = lax.rem(lax.div(grp, 2), 4)
    z = lax.div(grp, 8)
    def turn(value, by):
        return lax.rem(value + by, 4)

    lower = lax.rem(level + LEVELS - 1, LEVELS)
    upper = lax.rem(level + 1, LEVELS)
    along_y = {OWN: core == 0, ABOVE: core == 1, DOWN: core == 1}
    place_a = {panel: jnp.where(first, y, z) for panel, first in along_y.items()}
    place_b = {panel: jnp.where(first, z, y) for panel, first in along_y.items()}

    def device(panel, at_level, at_a, at_b):
        at_y = jnp.where(along_y[panel], at_a, at_b)
        at_z = jnp.where(along_y[panel], at_b, at_a)
        return (at_level, at_z * 8 + at_y * 2 + core)

    def around(panel, at_level, by_a, by_b):
        return device(panel, at_level, turn(place_a[panel], by_a), turn(place_b[panel], by_b))

    sibling = (level, z * 8 + y * 2 + 1 - core)

    loads = [
        (x_hbm.at[0], x_vmem),
        (level_hbm.at[0], level_t),
        (up_hbm.at[0], up),
        (rhs_hbm.at[0, :, pl.ds(0, 8), :], rhs_vmem.at[0]),
        (rhs_hbm.at[0, :, pl.ds(8, 8), :], rhs_vmem.at[1]),
        (inv_hbm.at[0], inv),
        (down_hbm.at[0], down),
    ]
    loads = [pltpu.make_async_copy(src, dst, load_sem.at[n]) for n, (src, dst) in enumerate(loads)]
    for load in loads:
        load.start()

    barrier = pltpu.get_barrier_semaphore()
    partners = [sibling]
    partners += [around(OWN, level, d, 0) for d in (1, 2, 3)]
    partners += [around(OWN, level, 0, d) for d in (1, 2, 3)]
    partners += [around(ABOVE, lower, d, 0) for d in (0, 1, 2, 3)]
    partners += [around(DOWN, upper, d, 0) for d in (0, 1, 2, 3)]
    for partner in partners:
        pl.semaphore_signal(barrier, inc=1, device_id=partner, device_id_type=MESH)

    def shard_at(panel, by_a):
        return (core * 16 + place_b[panel] * 4 + turn(place_a[panel], by_a)) * SHARD

    def shard(panel, by_a=0):
        return pl.ds(shard_at(panel, by_a), SHARD)

    def group(panel, by_b):
        return pl.ds((core * 16 + turn(place_b[panel], by_b) * 4) * SHARD, GROUP)

    def half(at_core):
        return pl.ds(at_core * HALF, HALF)

    def recv(panel, part, which):
        return recv_sem.at[(panel * PARTS + part) * 8 + which]

    def sent(panel, part, which):
        return send_sem.at[(panel * PARTS + part) * 4 + which]

    def spread(source, panel, part, target, turns):
        for d in turns:
            pltpu.make_async_remote_copy(
                src_ref=source,
                dst_ref=panels[panel].at[part, shard(panel)],
                send_sem=sent(panel, part, 0),
                recv_sem=recv(panel, part, d),
                device_id=around(panel, target, d, 0),
                device_id_type=MESH,
            ).start()

    def wait_bytes(ref, sem):
        pltpu.make_async_copy(ref, ref, sem).wait()

    def to_sibling(panel, part, which):
        ref = panels[panel].at[part].at[which]
        pltpu.make_async_remote_copy(
            src_ref=ref,
            dst_ref=ref,
            send_sem=sent(panel, part, 2),
            recv_sem=recv(panel, part, 4),
            device_id=sibling,
            device_id_type=MESH,
        ).start()

    def send_on(panel, part, by_a):
        ref = panels[panel].at[part, shard(panel, by_a)]
        for d in S2_ORDER:
            pltpu.make_async_remote_copy(
                src_ref=ref,
                dst_ref=ref,
                send_sem=sent(panel, part, 1),
                recv_sem=recv(panel, part, 4 + d),
                device_id=around(panel, level, 0, d),
                device_id_type=MESH,
            ).start()

    def relay(panel, part):
        for d in (1, 3, 2) if panel == OWN else (0, 1, 3, 2):
            wait_bytes(panels[panel].at[part, shard(panel, 4 - d)], recv(panel, part, d))
            send_on(panel, part, 4 - d)
        to_sibling(panel, part, group(panel, 0))

    def share(panel, part):
        for d in (1, 3, 2):
            theirs = group(panel, 4 - d)
            wait_bytes(panels[panel].at[part, theirs], recv(panel, part, 4 + d))
            to_sibling(panel, part, theirs)

    def complete(panel, part):
        wait_bytes(panels[panel].at[part].at[half(1 - core)], recv(panel, part, 4))

    def drain(panel, part, shards):
        ref = panels[panel].at[part]
        wait_bytes(ref.at[pl.ds(0, shards * SHARD)], sent(panel, part, 0))

    def drain_rest(panel, part):
        ref = panels[panel].at[part]
        wait_bytes(ref.at[pl.ds(0, 3 * GROUP)], sent(panel, part, 1))
        wait_bytes(ref.at[pl.ds(0, 4 * GROUP)], sent(panel, part, 2))

    row_group = lax.broadcasted_iota(jnp.int32, (ROWS, TILE), 0) // WIDTH
    for q in range(PARTS + 1):
        masks[q] = jnp.where(row_group == q, 1.0, 0.0).astype(BF16)

    def index_row(i, carry):
        for band in range(3):
            count = counts[band, 0, i]
            if band == ABOVE:
                count = jnp.where(level == LEVELS - 1, 0, count)
            for k in range(SLOTS):
                col = cols[band, k, 0, i]
                owner, j = lax.shift_right_logical(col, 4), lax.bitwise_and(col, 15)
                oz = lax.shift_right_logical(owner, 3)
                oy = lax.bitwise_and(lax.shift_right_logical(owner, 1), 3)
                even = lax.bitwise_and(owner, 1) == 0
                pos = jnp.where(even, 0, 16) + jnp.where(
                    even == (band == OWN), oz * 4 + oy, oy * 4 + oz
                )
                place[band, i * SLOTS + k] = pos * SHARD + j // PARTS
                pick[band, i * SLOTS + k] = jnp.where(k < count, lax.rem(j, PARTS), PARTS)
        return carry

    lax.fori_loop(0, ROWS, index_row, 0)

    loads[0].wait()
    for part in range(PARTS):
        for j in range(SHARD):
            rows = [
                x_vmem[PARTS * j + q].astype(F32)[part * WIDTH : (part + 1) * WIDTH]
                for q in range(PARTS)
            ]
            panels[OWN][part, shard_at(OWN, 0) + j] = jnp.concatenate(rows, axis=0).astype(BF16)

    pl.semaphore_wait(barrier, len(partners))
    for part in range(PARTS):
        mine = panels[OWN].at[part, shard(OWN)]
        spread(mine, OWN, part, level, (2, 1, 3))

        @pl.when(level > 0)
        def _():
            spread(mine, ABOVE, part, lower, (2, 1, 3, 0))

        send_on(OWN, part, 0)

    loads[5].wait()

    def split_row(i, carry):
        whole = inv[i]
        high = whole.astype(BF16)
        inv_split[i, :, :TILE] = high
        inv_split[i, :, TILE:] = (whole - high.astype(F32)).astype(BF16)
        return carry

    lax.fori_loop(0, ROWS, split_row, 0)

    def band_term(band, tiles, blocks, i):
        pieces = [
            blocks[place[band, i * SLOTS + k]] * masks[pick[band, i * SLOTS + k]]
            for k in range(SLOTS)
        ]
        left = jnp.concatenate(pieces, axis=1)
        right = tiles[i].reshape(SLOTS * TILE, TILE)
        return jnp.dot(left, right, preferred_element_type=F32)

    def solve(rest, i):
        high = rest.astype(BF16).astype(F32)
        both = jnp.concatenate([high, rest - high], axis=0).astype(BF16)
        four = jnp.dot(both, inv_split[i], preferred_element_type=F32)
        two = four[:, :TILE] + four[:, TILE:]
        return two[:WIDTH] + two[WIDTH:]

    def all_rows(step):
        if STEP == ROWS:
            step(0)
        else:
            lax.fori_loop(0, ROWS // STEP, lambda n, carry: (step(n), carry)[1], 0)

    def base_rows(turn_, sub, part):
        def step(n):
            for m in range(STEP):
                i = n * STEP + m
                total = band_term(OWN, level_t, work, i) + band_term(ABOVE, up, work_above, i)
                rhs = rhs_vmem[turn_, i, sub * WIDTH : (sub + 1) * WIDTH, :]
                bases[part, i] = rhs - fold(total)

        all_rows(step)

    def down_rows(part):
        def step(n):
            for m in range(STEP):
                i = n * STEP + m
                resid[i] = bases[part, i] - fold(band_term(DOWN, down, work, i))

        all_rows(step)

    def finish(turn_, sub, part, rest_of):
        def step(n):
            done = []
            for m in range(STEP):
                i = n * STEP + m
                result = solve(rest_of(i), i)
                results[turn_, i, sub * WIDTH : (sub + 1) * WIDTH, :] = result
                done.append(result)
            for m in range(STEP // PARTS):
                tile = jnp.concatenate(done[m * PARTS : (m + 1) * PARTS], axis=0)
                outgoing[part, n * (STEP // PARTS) + m] = tile.astype(BF16)

        all_rows(step)

        @pl.when(level < LEVELS - 1)
        def _():
            spread(outgoing.at[part], DOWN, part, upper, S1_ORDER)

    def relay_both(part):
        relay(OWN, part)

        @pl.when(level < LEVELS - 1)
        def _():
            relay(ABOVE, part)

    def share_both(part):
        share(OWN, part)

        @pl.when(level < LEVELS - 1)
        def _():
            share(ABOVE, part)

    for part in range(AHEAD):
        relay_both(part)

    @pl.when(level == LEVELS - 1)
    def _():
        work_above[...] = jnp.zeros_like(work_above)

    for n in (1, 2, 3, 4):
        loads[n].wait()

    def base_turn(turn_, carry):
        for sub in range(SUBS):
            part = turn_ * SUBS + sub

            @pl.when(part + AHEAD < PARTS)
            def _():
                relay_both(part + AHEAD)

            @pl.when(part <= BASE_FROM)
            def _():
                share_both(part)

            @pl.when((part >= BASE_FROM) & (part + 1 < PARTS))
            def _():
                share_both(part + 1)

            complete(OWN, part)
            work[...] = panel_own[part]

            @pl.when(level < LEVELS - 1)
            def _():
                complete(ABOVE, part)
                work_above[...] = panel_above[part]

            base_rows(turn_, sub, part)

            @pl.when(level == 0)
            def _():
                finish(turn_, sub, part, lambda i: bases[part, i])

            @pl.when((level == 1) & (part >= BETWEEN))
            def _():
                relay(DOWN, part - BETWEEN)

        return carry

    lax.fori_loop(0, TURNS, base_turn, 0)
    loads[6].wait()

    @pl.when(level > 0)
    def _():
        @pl.when(level > 1)
        def _():
            for part in range(LATE_AHEAD):
                relay(DOWN, part)

        def down_turn(turn_, carry):
            for sub in range(SUBS):
                part = turn_ * SUBS + sub

                later = part + jnp.where(level > 1, LATE_AHEAD, DOWN_AHEAD)

                @pl.when((later < PARTS) & ((level > 1) | (later >= PARTS - BETWEEN)))
                def _():
                    relay(DOWN, later)

                share(DOWN, part)
                complete(DOWN, part)
                work[...] = panel_down[part]
                down_rows(part)
                finish(turn_, sub, part, lambda i: resid[i])

            return carry

        lax.fori_loop(0, TURNS, down_turn, 0)

    for turn_ in range(TURNS):
        out_ref[0, :, turn_ * 8 : (turn_ + 1) * 8, :] = results[turn_]
    for part in range(PARTS):
        drain(OWN, part, 3)
        drain_rest(OWN, part)

        @pl.when(level < LEVELS - 1)
        def _():
            drain(DOWN, part, 4)
            drain_rest(ABOVE, part)

        @pl.when(level > 0)
        def _():
            drain(ABOVE, part, 4)
            drain_rest(DOWN, part)


def shards(x_old, rhs, down_tiles, level_tiles, up_tiles, inverses, tile_cols, tile_counts):
    cols = tile_cols.transpose(2, 3, 0, 1)
    counts = tile_counts.transpose(2, 0, 1)
    in_hbm = pl.BlockSpec(memory_space=pltpu.HBM)
    in_smem = pl.BlockSpec(memory_space=pltpu.SMEM)
    panel = pltpu.VMEM((PARTS, 32 * SHARD, ROWS, TILE), BF16)
    return pl.pallas_call(
        sweep,
        out_shape=pltpu.VMEM(rhs.shape, F32),
        in_specs=[in_hbm] * 6 + [in_smem] * 2,
        out_specs=pl.BlockSpec(memory_space=pltpu.VMEM),
        scratch_shapes=[panel] * 3
        + [
            pltpu.VMEM((32 * SHARD, ROWS, TILE), BF16),
            pltpu.VMEM((32 * SHARD, ROWS, TILE), BF16),
            pltpu.VMEM((PARTS, SHARD, ROWS, TILE), BF16),
            pltpu.VMEM((TURNS, ROWS, 8, TILE), F32),
            pltpu.VMEM((PARTS, ROWS, WIDTH, TILE), F32),
            pltpu.VMEM((ROWS, WIDTH, TILE), F32),
            pltpu.VMEM((ROWS, ROWS, TILE), BF16),
            pltpu.VMEM((TURNS, ROWS, 8, TILE), F32),
            pltpu.VMEM((ROWS, SLOTS, TILE, TILE), BF16),
            pltpu.VMEM((ROWS, SLOTS, TILE, TILE), BF16),
            pltpu.VMEM((ROWS, SLOTS, TILE, TILE), BF16),
            pltpu.VMEM((ROWS, TILE, TILE), F32),
            pltpu.VMEM((ROWS, TILE, 2 * TILE), BF16),
            pltpu.VMEM((PARTS + 1, ROWS, TILE), BF16),
            pltpu.SMEM((3, ROWS * SLOTS), jnp.int32),
            pltpu.SMEM((3, ROWS * SLOTS), jnp.int32),
            pltpu.SemaphoreType.DMA((7,)),
            pltpu.SemaphoreType.DMA((3 * PARTS * 4,)),
            pltpu.SemaphoreType.DMA((3 * PARTS * 8,)),
        ],
        compiler_params=pltpu.CompilerParams(
            collective_id=0, has_side_effects=True, vmem_limit_bytes=60 * 1024 * 1024
        ),
        name="sweep",
    )(x_old, rhs, down_tiles, level_tiles, up_tiles, inverses, cols, counts)


def solution(mesh):
    return jax.shard_map(
        shards,
        mesh=mesh,
        in_specs=(
            P("level", "grp", None, None),
            P("level", "grp", None, None),
            P("level", "grp", None, None, None),
            P("level", "grp", None, None, None),
            P("level", "grp", None, None, None),
            P("level", "grp", None, None),
            P("level", "grp", None, None),
            P("level", "grp", None),
        ),
        out_specs=P("level", "grp", None, None),
        check_vma=False,
    )
```

```python
import jax
import jax.numpy as jnp
from jax import lax
from jax.experimental import pallas as pl
from jax.experimental.pallas import tpu as pltpu
from jax.sharding import PartitionSpec as P

MESH = pl.DeviceIdType.MESH
ROWS = 16
SLOTS = 6
TILE = 128
LEVELS = 4
PARTS = 4
WIDTH = ROWS // PARTS
SHARD = ROWS // PARTS
GROUP = 4 * SHARD
HALF = 16 * SHARD
TURNS = 2
SUBS = PARTS // TURNS
STEP = 16
OWN, ABOVE, DOWN = 1, 2, 0
AHEAD = 4
DOWN_AHEAD = 2
LATE_AHEAD = 2
BETWEEN = 1
S2_ORDER = (2, 1, 3)
S1_ORDER = (2, 1, 3, 0)
BASE_FROM = 1
F32, BF16 = jnp.float32, jnp.bfloat16


def fold(total):
    while total.shape[0] > WIDTH:
        half = total.shape[0] // 2
        total = total[:half] + total[half:]
    return total


def sweep(
    x_hbm, rhs_hbm, down_hbm, level_hbm, up_hbm, inv_hbm, cols, counts, out_ref,
    panel_down, panel_own, panel_above, work, work_above, outgoing, results, bases, resid,
    x_vmem, rhs_vmem, down, level_t, up, inv, inv_split, masks, place, pick,
    load_sem, send_sem, recv_sem,
):
    panels = {DOWN: panel_down, OWN: panel_own, ABOVE: panel_above}
    level = lax.axis_index("level")
    grp = lax.axis_index("grp")
    core = lax.rem(grp, 2)
    y = lax.rem(lax.div(grp, 2), 4)
    z = lax.div(grp, 8)
    def turn(value, by):
        return lax.rem(value + by, 4)

    lower = lax.rem(level + LEVELS - 1, LEVELS)
    upper = lax.rem(level + 1, LEVELS)
    along_y = {OWN: core == 0, ABOVE: core == 1, DOWN: core == 1}
    place_a = {panel: jnp.where(first, y, z) for panel, first in along_y.items()}
    place_b = {panel: jnp.where(first, z, y) for panel, first in along_y.items()}

    def device(panel, at_level, at_a, at_b):
        at_y = jnp.where(along_y[panel], at_a, at_b)
        at_z = jnp.where(along_y[panel], at_b, at_a)
        return (at_level, at_z * 8 + at_y * 2 + core)

    def around(panel, at_level, by_a, by_b):
        return device(panel, at_level, turn(place_a[panel], by_a), turn(place_b[panel], by_b))

    sibling = (level, z * 8 + y * 2 + 1 - core)

    loads = [
        (x_hbm.at[0], x_vmem),
        (level_hbm.at[0], level_t),
        (up_hbm.at[0], up),
        (rhs_hbm.at[0, :, pl.ds(0, 8), :], rhs_vmem.at[0]),
        (rhs_hbm.at[0, :, pl.ds(8, 8), :], rhs_vmem.at[1]),
        (inv_hbm.at[0], inv),
        (down_hbm.at[0], down),
    ]
    loads = [pltpu.make_async_copy(src, dst, load_sem.at[n]) for n, (src, dst) in enumerate(loads)]
    for load in loads:
        load.start()

    barrier = pltpu.get_barrier_semaphore()
    partners = [sibling]
    partners += [around(OWN, level, d, 0) for d in (1, 2, 3)]
    partners += [around(OWN, level, 0, d) for d in (1, 2, 3)]
    partners += [around(ABOVE, lower, d, 0) for d in (0, 1, 2, 3)]
    partners += [around(DOWN, upper, d, 0) for d in (0, 1, 2, 3)]
    for partner in partners:
        pl.semaphore_signal(barrier, inc=1, device_id=partner, device_id_type=MESH)

    def shard_at(panel, by_a):
        return (core * 16 + place_b[panel] * 4 + turn(place_a[panel], by_a)) * SHARD

    def shard(panel, by_a=0):
        return pl.ds(shard_at(panel, by_a), SHARD)

    def group(panel, by_b):
        return pl.ds((core * 16 + turn(place_b[panel], by_b) * 4) * SHARD, GROUP)

    def half(at_core):
        return pl.ds(at_core * HALF, HALF)

    def recv(panel, part, which):
        return recv_sem.at[(panel * PARTS + part) * 8 + which]

    def sent(panel, part, which):
        return send_sem.at[(panel * PARTS + part) * 4 + which]

    def spread(source, panel, part, target, turns):
        for d in turns:
            pltpu.make_async_remote_copy(
                src_ref=source,
                dst_ref=panels[panel].at[part, shard(panel)],
                send_sem=sent(panel, part, 0),
                recv_sem=recv(panel, part, d),
                device_id=around(panel, target, d, 0),
                device_id_type=MESH,
            ).start()

    def wait_bytes(ref, sem):
        pltpu.make_async_copy(ref, ref, sem).wait()

    def to_sibling(panel, part, which):
        ref = panels[panel].at[part].at[which]
        pltpu.make_async_remote_copy(
            src_ref=ref,
            dst_ref=ref,
            send_sem=sent(panel, part, 2),
            recv_sem=recv(panel, part, 4),
            device_id=sibling,
            device_id_type=MESH,
        ).start()

    def send_on(panel, part, by_a):
        ref = panels[panel].at[part, shard(panel, by_a)]
        for d in S2_ORDER:
            pltpu.make_async_remote_copy(
                src_ref=ref,
                dst_ref=ref,
                send_sem=sent(panel, part, 1),
                recv_sem=recv(panel, part, 4 + d),
                device_id=around(panel, level, 0, d),
                device_id_type=MESH,
            ).start()

    def relay(panel, part):
        for d in (1, 3, 2) if panel == OWN else (0, 1, 3, 2):
            wait_bytes(panels[panel].at[part, shard(panel, 4 - d)], recv(panel, part, d))
            send_on(panel, part, 4 - d)
        to_sibling(panel, part, group(panel, 0))

    def share(panel, part):
        for d in (1, 3, 2):
            theirs = group(panel, 4 - d)
            wait_bytes(panels[panel].at[part, theirs], recv(panel, part, 4 + d))
            to_sibling(panel, part, theirs)

    def complete(panel, part):
        wait_bytes(panels[panel].at[part].at[half(1 - core)], recv(panel, part, 4))

    def drain(panel, part, shards):
        ref = panels[panel].at[part]
        wait_bytes(ref.at[pl.ds(0, shards * SHARD)], sent(panel, part, 0))

    def drain_rest(panel, part):
        ref = panels[panel].at[part]
        wait_bytes(ref.at[pl.ds(0, 3 * GROUP)], sent(panel, part, 1))
        wait_bytes(ref.at[pl.ds(0, 4 * GROUP)], sent(panel, part, 2))

    row_group = lax.broadcasted_iota(jnp.int32, (ROWS, TILE), 0) // WIDTH
    for q in range(PARTS + 1):
        masks[q] = jnp.where(row_group == q, 1.0, 0.0).astype(BF16)

    def index_row(i, carry):
        for band in range(3):
            count = counts[band, 0, i]
            if band == ABOVE:
                count = jnp.where(level == LEVELS - 1, 0, count)
            for k in range(SLOTS):
                col = cols[band, k, 0, i]
                owner, j = lax.shift_right_logical(col, 4), lax.bitwise_and(col, 15)
                oz = lax.shift_right_logical(owner, 3)
                oy = lax.bitwise_and(lax.shift_right_logical(owner, 1), 3)
                even = lax.bitwise_and(owner, 1) == 0
                pos = jnp.where(even, 0, 16) + jnp.where(
                    even == (band == OWN), oz * 4 + oy, oy * 4 + oz
                )
                place[band, i * SLOTS + k] = pos * SHARD + j // PARTS
                pick[band, i * SLOTS + k] = jnp.where(k < count, lax.rem(j, PARTS), PARTS)
        return carry

    lax.fori_loop(0, ROWS, index_row, 0)

    loads[0].wait()
    for part in range(PARTS):
        for j in range(SHARD):
            rows = [
                x_vmem[PARTS * j + q].astype(F32)[part * WIDTH : (part + 1) * WIDTH]
                for q in range(PARTS)
            ]
            panels[OWN][part, shard_at(OWN, 0) + j] = jnp.concatenate(rows, axis=0).astype(BF16)

    pl.semaphore_wait(barrier, len(partners))
    for part in range(PARTS):
        mine = panels[OWN].at[part, shard(OWN)]
        spread(mine, OWN, part, level, (2, 1, 3))

        @pl.when(level > 0)
        def _():
            spread(mine, ABOVE, part, lower, (2, 1, 3, 0))

        send_on(OWN, part, 0)

    loads[5].wait()

    def split_row(i, carry):
        whole = inv[i]
        high = whole.astype(BF16)
        inv_split[i, :, :TILE] = high
        inv_split[i, :, TILE:] = (whole - high.astype(F32)).astype(BF16)
        return carry

    lax.fori_loop(0, ROWS, split_row, 0)

    def band_term(band, tiles, blocks, i):
        pieces = [
            blocks[place[band, i * SLOTS + k]] * masks[pick[band, i * SLOTS + k]]
            for k in range(SLOTS)
        ]
        left = jnp.concatenate(pieces, axis=1)
        right = tiles[i].reshape(SLOTS * TILE, TILE)
        return jnp.dot(left, right, preferred_element_type=F32)

    def solve(rest, i):
        high = rest.astype(BF16).astype(F32)
        both = jnp.concatenate([high, rest - high], axis=0).astype(BF16)
        four = jnp.dot(both, inv_split[i], preferred_element_type=F32)
        two = four[:, :TILE] + four[:, TILE:]
        return two[:WIDTH] + two[WIDTH:]

    def all_rows(step):
        if STEP == ROWS:
            step(0)
        else:
            lax.fori_loop(0, ROWS // STEP, lambda n, carry: (step(n), carry)[1], 0)

    def base_rows(turn_, sub, part):
        def step(n):
            for m in range(STEP):
                i = n * STEP + m
                total = band_term(OWN, level_t, work, i) + band_term(ABOVE, up, work_above, i)
                rhs = rhs_vmem[turn_, i, sub * WIDTH : (sub + 1) * WIDTH, :]
                bases[part, i] = rhs - fold(total)

        all_rows(step)

    def down_rows(part):
        def step(n):
            for m in range(STEP):
                i = n * STEP + m
                resid[i] = bases[part, i] - fold(band_term(DOWN, down, work, i))

        all_rows(step)

    def finish(turn_, sub, part, rest_of):
        def step(n):
            done = []
            for m in range(STEP):
                i = n * STEP + m
                result = solve(rest_of(i), i)
                results[turn_, i, sub * WIDTH : (sub + 1) * WIDTH, :] = result
                done.append(result)
            for m in range(STEP // PARTS):
                tile = jnp.concatenate(done[m * PARTS : (m + 1) * PARTS], axis=0)
                outgoing[part, n * (STEP // PARTS) + m] = tile.astype(BF16)

        all_rows(step)

        @pl.when(level < LEVELS - 1)
        def _():
            spread(outgoing.at[part], DOWN, part, upper, S1_ORDER)

    def relay_both(part):
        relay(OWN, part)

        @pl.when(level < LEVELS - 1)
        def _():
            relay(ABOVE, part)

    def share_both(part):
        share(OWN, part)

        @pl.when(level < LEVELS - 1)
        def _():
            share(ABOVE, part)

    for part in range(AHEAD):
        relay_both(part)

    @pl.when(level == LEVELS - 1)
    def _():
        work_above[...] = jnp.zeros_like(work_above)

    for n in (1, 2, 3, 4):
        loads[n].wait()

    def base_turn(turn_, carry):
        for sub in range(SUBS):
            part = turn_ * SUBS + sub

            @pl.when(part + AHEAD < PARTS)
            def _():
                relay_both(part + AHEAD)

            @pl.when(part <= BASE_FROM)
            def _():
                share_both(part)

            @pl.when((part >= BASE_FROM) & (part + 1 < PARTS))
            def _():
                share_both(part + 1)

            complete(OWN, part)
            work[...] = panel_own[part]

            @pl.when(level < LEVELS - 1)
            def _():
                complete(ABOVE, part)
                work_above[...] = panel_above[part]

            base_rows(turn_, sub, part)

            @pl.when(level == 0)
            def _():
                finish(turn_, sub, part, lambda i: bases[part, i])

            @pl.when((level == 1) & (part >= BETWEEN))
            def _():
                relay(DOWN, part - BETWEEN)

        return carry

    lax.fori_loop(0, TURNS, base_turn, 0)
    loads[6].wait()

    @pl.when(level > 0)
    def _():
        @pl.when(level > 1)
        def _():
            for part in range(LATE_AHEAD):
                relay(DOWN, part)

        def down_turn(turn_, carry):
            for sub in range(SUBS):
                part = turn_ * SUBS + sub

                later = part + jnp.where(level > 1, LATE_AHEAD, DOWN_AHEAD)

                @pl.when((later < PARTS) & ((level > 1) | (later >= PARTS - BETWEEN)))
                def _():
                    relay(DOWN, later)

                share(DOWN, part)
                complete(DOWN, part)
                work[...] = panel_down[part]
                down_rows(part)
                finish(turn_, sub, part, lambda i: resid[i])

            return carry

        lax.fori_loop(0, TURNS, down_turn, 0)

    for turn_ in range(TURNS):
        out_ref[0, :, turn_ * 8 : (turn_ + 1) * 8, :] = results[turn_]
    for part in range(PARTS):
        drain(OWN, part, 3)
        drain_rest(OWN, part)

        @pl.when(level < LEVELS - 1)
        def _():
            drain(DOWN, part, 4)
            drain_rest(ABOVE, part)

        @pl.when(level > 0)
        def _():
            drain(ABOVE, part, 4)
            drain_rest(DOWN, part)


def shards(x_old, rhs, down_tiles, level_tiles, up_tiles, inverses, tile_cols, tile_counts):
    cols = tile_cols.transpose(2, 3, 0, 1)
    counts = tile_counts.transpose(2, 0, 1)
    in_hbm = pl.BlockSpec(memory_space=pltpu.HBM)
    in_smem = pl.BlockSpec(memory_space=pltpu.SMEM)
    panel = pltpu.VMEM((PARTS, 32 * SHARD, ROWS, TILE), BF16)
    return pl.pallas_call(
        sweep,
        out_shape=pltpu.VMEM(rhs.shape, F32),
        in_specs=[in_hbm] * 6 + [in_smem] * 2,
        out_specs=pl.BlockSpec(memory_space=pltpu.VMEM),
        scratch_shapes=[panel] * 3
        + [
            pltpu.VMEM((32 * SHARD, ROWS, TILE), BF16),
            pltpu.VMEM((32 * SHARD, ROWS, TILE), BF16),
            pltpu.VMEM((PARTS, SHARD, ROWS, TILE), BF16),
            pltpu.VMEM((TURNS, ROWS, 8, TILE), F32),
            pltpu.VMEM((PARTS, ROWS, WIDTH, TILE), F32),
            pltpu.VMEM((ROWS, WIDTH, TILE), F32),
            pltpu.VMEM((ROWS, ROWS, TILE), BF16),
            pltpu.VMEM((TURNS, ROWS, 8, TILE), F32),
            pltpu.VMEM((ROWS, SLOTS, TILE, TILE), BF16),
            pltpu.VMEM((ROWS, SLOTS, TILE, TILE), BF16),
            pltpu.VMEM((ROWS, SLOTS, TILE, TILE), BF16),
            pltpu.VMEM((ROWS, TILE, TILE), F32),
            pltpu.VMEM((ROWS, TILE, 2 * TILE), BF16),
            pltpu.VMEM((PARTS + 1, ROWS, TILE), BF16),
            pltpu.SMEM((3, ROWS * SLOTS), jnp.int32),
            pltpu.SMEM((3, ROWS * SLOTS), jnp.int32),
            pltpu.SemaphoreType.DMA((7,)),
            pltpu.SemaphoreType.DMA((3 * PARTS * 4,)),
            pltpu.SemaphoreType.DMA((3 * PARTS * 8,)),
        ],
        compiler_params=pltpu.CompilerParams(
            collective_id=0, has_side_effects=True, vmem_limit_bytes=60 * 1024 * 1024
        ),
        name="sweep",
    )(x_old, rhs, down_tiles, level_tiles, up_tiles, inverses, cols, counts)


def solution(mesh):
    return jax.shard_map(
        shards,
        mesh=mesh,
        in_specs=(
            P("level", "grp", None, None),
            P("level", "grp", None, None),
            P("level", "grp", None, None, None),
            P("level", "grp", None, None, None),
            P("level", "grp", None, None, None),
            P("level", "grp", None, None),
            P("level", "grp", None, None),
            P("level", "grp", None),
        ),
        out_specs=P("level", "grp", None, None),
        check_vma=False,
    )
```
